32 devices in a mesh: lon: 16 (over z, y, core), lat: 2 (over x).
Axes of the slice: x: 2, y: 2, z: 4, core: 2. Of those that a mesh axis runs over, the one named last changes fastest.
Arguments:
- pressure: float32 [128, 256, 256], P(None, 'lon', 'lat'), may hold values from -10 to 10
- ocean_mask: int32 [256, 256], P('lon', 'lat'), may hold values 0 or 1
Outputs:
- modes: float32 [128, 3, 256, 256], P(None, None, 'lon', 'lat')
- factor_r: float32 [128, 128], replicated
The draws below stay inside these ranges and needn't reach their ends.
All inputs are finite; a program needn't handle non-finite values. No bound on the sum of `ocean_mask` on one device may be relied on, other than what follows from the above.
Results may differ from the reference program's by a relative error of at most 0.0003.
Values sent between devices are 32-bit elements; how exact they have to be, the bound alone decides.
No kernel may reach another device: no remote copies, remote signals or barrier semaphores. Data moves between devices by JAX's collectives and lax.ppermute only.
A program may use at most 64 MiB of HBM per device.

```python
import math
import jax
import jax.numpy as jnp
from jax import lax

SNAPS = 128
PASSES = 4
NLON = 256
NLAT = 256
ROWS = 196608


def draw_pressure(key, part):
    subkeys = jax.random.split(jax.random.fold_in(key, 7919), 4)
    pattern_count = 6
    longitude = jnp.arange(NLON, dtype=jnp.float32)[:, None]
    latitude = jnp.arange(NLAT, dtype=jnp.float32)[None, :]
    chosen = jax.random.permutation(subkeys[0], 12)[:pattern_count]
    wave_lon = (chosen % 4 + 1).astype(jnp.float32)
    wave_lat = (chosen // 4 + 1).astype(jnp.float32)
    phases = jax.random.uniform(subkeys[1], (pattern_count, 2), jnp.float32, -math.pi, math.pi)
    decay_rate = 0.6 ** jnp.arange(pattern_count, dtype=jnp.float32)
    amplitude = jax.random.truncated_normal(subkeys[2], -4.0, 4.0, (SNAPS, pattern_count), jnp.float32)
    noise_field = 0.05 * jax.random.truncated_normal(subkeys[3], -4.0, 4.0, (SNAPS, NLON, NLAT), jnp.float32)
    summed = noise_field
    for which in range(pattern_count):
        along_lon = jnp.cos(2.0 * math.pi * wave_lon[which] * longitude / NLON + phases[which, 0])
        along_lat = jnp.cos(math.pi * wave_lat[which] * (latitude + 0.5) / NLAT + phases[which, 1])
        pattern = along_lon * along_lat
        weight_row = decay_rate[which] * amplitude[:, which]
        summed = summed + weight_row[:, None, None] * pattern[None, :, :]
    return summed.astype(jnp.float32)


def with_ends(result, key, low, top_value):
    longest = result.shape.index(max(result.shape))
    spots = []
    for shift in (0, 1):
        where = [jax.random.randint(jax.random.fold_in(key, axis), (), 0, length) for axis, length in enumerate(result.shape)]
        where[longest] = (where[longest] + shift) % result.shape[longest]
        spots.append(tuple(where))
    return result.at[spots[0]].set(low).at[spots[1]].set(top_value)


def setup_inputs(seed: int = 0) -> dict:
    seeds = jax.random.split(jax.random.key(seed), 3)
    return {
        "pressure": draw_pressure(jax.random.fold_in(seeds[2], 71), 0),
        "ocean_mask": with_ends((jax.random.randint(seeds[1], (NLON, NLAT), 0, 10) < 7).astype(jnp.int32), jax.random.fold_in(seeds[1], 1), 0, 1),
    }


def sweep_lon(field, mask):
    left = jnp.roll(field, 1, axis=1)
    right = jnp.roll(field, -1, axis=1)
    mask_left = jnp.roll(mask, 1, axis=0)
    mask_right = jnp.roll(mask, -1, axis=0)
    return mask * (field + 0.25 * (mask_left * (left - field) + mask_right * (right - field)))

def sweep_lat(field, mask):
    padded = jnp.pad(field, ((0, 0), (0, 0), (1, 1)))
    mask_pad = jnp.pad(mask, ((0, 0), (1, 1)))
    left = padded[:, :, :-2]
    right = padded[:, :, 2:]
    return mask * (field + 0.25 * (mask_pad[:, :-2] * (left - field) + mask_pad[:, 2:] * (right - field)))

def orthonormalize(flat):
    gram = lax.dot_general(flat.astype(jnp.float32), flat.astype(jnp.float32), (((1,), (1,)), ((), ())), precision=lax.Precision.HIGHEST, preferred_element_type=jnp.float32)
    lower = jnp.linalg.cholesky(gram)
    eye = jnp.eye(gram.shape[0], dtype=jnp.float32)
    inverse = jax.scipy.linalg.solve_triangular(lower, eye, lower=True)
    return (jnp.dot(inverse.astype(jnp.float32), flat.astype(jnp.float32), precision=lax.Precision.HIGHEST, preferred_element_type=jnp.float32), lower)

def reference(pressure, ocean_mask):
    mask = ocean_mask.astype(jnp.float32)
    field = mask * pressure
    for step in range(PASSES):
        field = sweep_lon(field, mask)
        field = sweep_lat(field, mask)
    grad_lon = 0.5 * mask * (jnp.roll(field, -1, axis=1) - jnp.roll(field, 1, axis=1))
    padded = jnp.pad(field, ((0, 0), (0, 0), (1, 1)))
    grad_lat = 0.5 * mask * (padded[:, :, 2:] - padded[:, :, :-2])
    stacked = jnp.stack([field, grad_lon, grad_lat], axis=1)
    flat = stacked.reshape(SNAPS, -1)
    first, lower_one = orthonormalize(flat)
    second, lower_two = orthonormalize(first)
    scale = jnp.sqrt(jnp.float32(ROWS))
    modes = (second * scale).reshape(SNAPS, 3, NLON, NLAT)
    factor_r = jnp.dot(lower_two.T.astype(jnp.float32), lower_one.T.astype(jnp.float32), precision=lax.Precision.HIGHEST, preferred_element_type=jnp.float32) / scale
    return (modes, factor_r)
```

```python
import functools

import jax
import jax.numpy as jnp
from jax import lax
from jax.experimental import pallas as pl
from jax.experimental.pallas import tpu as pltpu
from jax.sharding import PartitionSpec as P

PASSES = 4
HALO = PASSES + 1
EDGE = 8
ROUND = 1.5 * 2.0**23
BOTH = ("lon", "lat")
HIGHEST = lax.Precision.HIGHEST


def power_of_two(value):
    scaled = value * (2.0**23 + 1.0)
    return scaled - (scaled - value)


def dot_nt(left, right):
    return lax.dot_general(
        left, right, (((1,), (1,)), ((), ())), preferred_element_type=jnp.float32
    )


def dot_nn(left, right, precision=None):
    return lax.dot_general(
        left,
        right,
        (((1,), (0,)), ((), ())),
        precision=precision,
        preferred_element_type=jnp.float32,
    )


def slices_of(scaled):
    first = (scaled + ROUND) - ROUND
    rest = (scaled - first) * 256.0
    second = (rest + ROUND) - ROUND
    rest = (rest - second) * 256.0
    third = (rest + ROUND) - ROUND
    return first, second, third


def prepare_kernel(pressure_ref, mask_ref, turned_ref, west_ref, east_ref, low_ref, high_ref, *, clon, clat, snaps):
    mask = mask_ref[...].astype(jnp.float32)
    for row in range(clon):
        plane = pressure_ref[pl.ds(row, snaps, stride=clon), :].T
        mask_rows = jnp.broadcast_to(mask[row : row + 1, :], (EDGE, clat))
        turned_ref[row] = plane
        low_ref[row, :EDGE] = plane[:EDGE]
        low_ref[row, EDGE:] = mask_rows
        high_ref[row, :EDGE] = plane[clat - EDGE :]
        high_ref[row, EDGE:] = mask_rows
        if row < HALO:
            west_ref[row, :clat] = plane
            west_ref[row, clat:] = mask_rows
        if row >= clon - HALO:
            east_ref[row - clon + HALO, :clat] = plane
            east_ref[row - clon + HALO, clat:] = mask_rows


def prepare(pressure, mask):
    snaps, clon, clat = pressure.shape
    flat = pressure.reshape(snaps * clon, clat)
    shapes = [
        (clon, clat, snaps),
        (HALO, clat + EDGE, snaps),
        (HALO, clat + EDGE, snaps),
        (clon, 2 * EDGE, snaps),
        (clon, 2 * EDGE, snaps),
    ]
    body = functools.partial(prepare_kernel, clon=clon, clat=clat, snaps=snaps)
    return pl.pallas_call(
        body,
        out_shape=[jax.ShapeDtypeStruct(shape, jnp.float32) for shape in shapes],
        name="prepare",
    )(flat, mask)


def extend(first, second, third, rows):
    pieces = [first, second, third]
    total = sum(piece.shape[0] for piece in pieces)
    if rows > total:
        pieces.append(jnp.zeros((rows - total, first.shape[1]), jnp.float32))
    return jnp.concatenate(pieces, axis=0)


def filter_kernel(
    side_ref,
    turned_ref,
    mask_ref,
    west_ref,
    east_ref,
    left_ref,
    left_west_ref,
    left_east_ref,
    right_ref,
    right_west_ref,
    right_east_ref,
    x_ref,
    gram_ref,
    field_a,
    field_b,
    swept,
    keep_lon,
    keep_lat,
    quarter,
    *,
    clon,
    clat,
    snaps,
):
    wide = clon + 2 * HALO
    tall = clat + 2 * EDGE
    padded = -(-wide // 8) * 8
    has_left = side_ref[0] > 0
    has_right = side_ref[1] > 0

    def if_left(value):
        return jnp.where(has_left, value, 0.0)

    def if_right(value):
        return jnp.where(has_right, value, 0.0)

    own = extend(west_ref[:, clat, :], mask_ref[...].astype(jnp.float32), east_ref[:, clat, :], padded)
    left = if_left(extend(left_west_ref[:, EDGE, :], left_ref[:, EDGE, :], left_east_ref[:, EDGE, :], padded))
    right = if_right(extend(right_west_ref[:, EDGE, :], right_ref[:, EDGE, :], right_east_ref[:, EDGE, :], padded))
    lane = lax.broadcasted_iota(jnp.int32, (padded, clat), 1)
    first_lane = lane == 0
    last_lane = lane == clat - 1

    def coefficients(mask, south, north):
        west_of = pltpu.roll(mask, 1, 0)
        east_of = pltpu.roll(mask, padded - 1, 0)
        return (
            mask * (1.0 - 0.25 * (west_of + east_of)),
            mask * (1.0 - 0.25 * (south + north)),
            0.25 * mask,
        )

    def up(mask):
        return pltpu.roll(mask, 1, 1)

    def down(mask):
        return pltpu.roll(mask, clat - 1, 1)

    own_c = coefficients(
        own,
        jnp.where(first_lane, up(left), up(own)),
        jnp.where(last_lane, down(right), down(own)),
    )
    left_c = coefficients(left, up(left), jnp.where(last_lane, down(own), down(left)))
    right_c = coefficients(right, jnp.where(first_lane, up(own), up(right)), down(right))
    columns = []
    for which in range(3):
        columns += [
            left_c[which].T[clat - EDGE :],
            own_c[which].T,
            right_c[which].T[:EDGE],
        ]
    columns = jnp.concatenate(columns, axis=0).astype(jnp.bfloat16)
    pick = lax.broadcasted_iota(jnp.int32, (padded, snaps), 0)

    zeros = jnp.zeros((EDGE, snaps), jnp.float32)
    lower, upper = EDGE, EDGE + tall

    def spread_row(row, carry):
        spread = dot_nn(columns, jnp.where(pick == row, 1.0, 0.0).astype(jnp.bfloat16))
        keep_lon[row] = spread[:tall]
        keep_lat[row] = spread[tall : 2 * tall]
        quarter[row] = spread[2 * tall :]
        swept[row, :lower] = zeros
        swept[row, upper:] = zeros
        return carry

    lax.fori_loop(0, wide, spread_row, 0)

    def place(row, low, middle, high):
        mask_row = quarter[row] * 4.0
        field_a[row, lower : lower + EDGE] = if_left(low) * mask_row[:EDGE]
        field_a[row, lower + EDGE : upper - EDGE] = middle * mask_row[EDGE : EDGE + clat]
        field_a[row, upper - EDGE : upper] = if_right(high) * mask_row[EDGE + clat :]

    for row in range(HALO):
        place(row, left_west_ref[row, :EDGE], west_ref[row, :clat], right_west_ref[row, :EDGE])
        place(
            HALO + clon + row,
            left_east_ref[row, :EDGE],
            east_ref[row, :clat],
            right_east_ref[row, :EDGE],
        )

    def place_own(row, carry):
        place(HALO + row, left_ref[row, :EDGE], turned_ref[row], right_ref[row, :EDGE])
        return carry

    lax.fori_loop(0, clon, place_own, 0)

    source, target = field_a, field_b
    for step in range(PASSES):

        def sweep(row, carry, source=source, target=target):
            around = source[row - 1, lower:upper] + source[row + 1, lower:upper]
            near = quarter[row]
            middle = keep_lon[row] * source[row, lower:upper] + near * around
            swept[row, lower:upper] = middle
            around = swept[row, lower - 1 : upper - 1] + swept[row, lower + 1 : upper + 1]
            target[row, lower:upper] = keep_lat[row] * middle + near * around
            return carry

        lax.fori_loop(step + 1, wide - 1 - step, sweep, 0)
        source, target = target, source

    begin, end = lower + EDGE, upper - EDGE

    def gradients(row, top):
        here = row + HALO
        center = source[here, begin:end]
        half = quarter[here, EDGE : EDGE + clat] * 2.0
        along_lon = half * (source[here + 1, begin:end] - source[here - 1, begin:end])
        along_lat = half * (source[here, begin + 1 : end + 1] - source[here, begin - 1 : end - 1])
        for which, value in enumerate((center, along_lon, along_lat)):
            value = value.T
            x_ref[which * clon + row] = value
            top = jnp.maximum(top, jnp.abs(value))
        return top

    top = lax.fori_loop(0, clon, gradients, jnp.zeros((snaps, clat), jnp.float32))
    unit = power_of_two(jnp.maximum(jnp.max(top, axis=1, keepdims=True), 2.0**-60))
    to_whole = jnp.broadcast_to(128.0 / unit, (snaps, clat))

    def multiply(pair, carry):
        whole, fine = carry
        exact = jnp.zeros((snaps, snaps), jnp.float32)
        for half in range(2):
            parts = [slices_of(x_ref[pair * 4 + half * 2 + which] * to_whole) for which in range(2)]
            first, second, third = [jnp.concatenate(both, axis=1) for both in zip(*parts)]
            a = first.astype(jnp.bfloat16)
            b = second.astype(jnp.bfloat16)
            c = third.astype(jnp.bfloat16)
            exact = exact + dot_nt(a, a)
            c_small = c * 2.0**-8
            fine = fine + (
                dot_nt(a, b)
                + dot_nt(a, c_small)
                + dot_nt(b * 2.0**-8, c_small)
                + dot_nt(b, b * 2.0**-9)
                + dot_nt(c, c * 2.0**-25)
            )
        return whole + exact.astype(jnp.int32), fine

    whole, fine = lax.fori_loop(
        0,
        3 * clon // 4,
        multiply,
        (jnp.zeros((snaps, snaps), jnp.int32), jnp.zeros((snaps, snaps), jnp.float32)),
    )
    head = whole.astype(jnp.float32)
    tail = (whole - head.astype(jnp.int32)).astype(jnp.float32) + (fine + fine.T) * 2.0**-8
    total = head + tail
    tail = tail - (total - head)
    unit = unit * (1.0 / 128.0)
    columns_unit = jnp.broadcast_to(unit, (snaps, snaps))
    rows_unit = columns_unit.T
    gram_ref[0] = total * columns_unit * rows_unit
    gram_ref[1] = tail * columns_unit * rows_unit


def filtered(side, turned, mask, halos):
    clon, clat, snaps = turned.shape
    wide = clon + 2 * HALO
    tall = clat + 2 * EDGE
    body = functools.partial(filter_kernel, clon=clon, clat=clat, snaps=snaps)
    vmem = pl.BlockSpec(memory_space=pltpu.VMEM)
    field = pltpu.VMEM((wide, tall + 2 * EDGE, snaps), jnp.float32)
    table = pltpu.VMEM((wide, tall, snaps), jnp.float32)
    return pl.pallas_call(
        body,
        out_shape=[
            jax.ShapeDtypeStruct((3 * clon, snaps, clat), jnp.float32),
            jax.ShapeDtypeStruct((2, snaps, snaps), jnp.float32),
        ],
        in_specs=[pl.BlockSpec(memory_space=pltpu.SMEM)] + [vmem] * 10,
        out_specs=[vmem, vmem],
        scratch_shapes=[field, field, field, table, table, table],
        compiler_params=pltpu.CompilerParams(vmem_limit_bytes=48 * 2**20),
        name="filter_and_gram",
    )(side, turned, mask, *halos)


def spread(row, lane):
    return jnp.broadcast_to(row[:, lane : lane + 1], row.shape)


def eliminate(tiles):
    count = len(tiles)
    size = tiles[0].shape[1]
    lane = lax.broadcasted_iota(jnp.int32, (8, size), 1)
    sub = lax.broadcasted_iota(jnp.int32, (8, size), 0)
    tiles = list(tiles)
    uppers, inverses = [], []
    for block in range(count):
        base = 8 * block
        panel = tiles[block]
        inside = (lane >= base) & (lane < base + 8)
        rows = [jnp.broadcast_to(panel[r : r + 1, :], (8, size)) for r in range(8)]
        entry = {(r, c): spread(rows[r], base + c) for r in range(8) for c in range(r + 1)}
        units = [jnp.where(lane == base + r, 1.0, 0.0) for r in range(8)]
        factor = {}
        pivots = []
        for k in range(8):
            pivots.append(1.0 / entry[k, k])
            for r in range(k + 1, 8):
                factor[r, k] = entry[r, k] * pivots[k]
            for r in range(k + 1, 8):
                for c in range(k + 1, r + 1):
                    entry[r, c] = entry[r, c] - factor[r, k] * entry[c, k]
        for k in range(8):
            for r in range(k + 1, 8):
                rows[r] = rows[r] - factor[r, k] * rows[k]
                units[r] = units[r] - factor[r, k] * units[k]
        joined = [jnp.where(inside, units[r], rows[r]) for r in range(8)]
        for i in range(block + 1, count):
            raw = [spread(tiles[i], base + k) for k in range(8)]
            tile = jnp.where(inside, 0.0, tiles[i])
            for k in range(8):
                scaled = raw[k] * pivots[k]
                for q in range(k + 1, 8):
                    raw[q] = raw[q] - scaled * entry[q, k]
                tile = tile - scaled * joined[k]
            tiles[i] = tile
        upper = jnp.zeros((8, size), jnp.float32)
        inverse = jnp.zeros((8, size), jnp.float32)
        for r in range(8):
            scale = lax.rsqrt(entry[r, r])
            upper = jnp.where(sub == r, rows[r] * scale, upper)
            inverse = jnp.where(sub == r, joined[r] * scale, inverse)
        uppers.append(jnp.where(lane >= base + sub, upper, 0.0))
        inverses.append(jnp.where(lane <= base + sub, inverse, 0.0))
    return jnp.concatenate(uppers, axis=0), jnp.concatenate(inverses, axis=0)


def tiles_of(matrix):
    return [matrix[8 * i : 8 * i + 8, :] for i in range(matrix.shape[0] // 8)]


def modes_kernel(gram_ref, x_ref, modes_ref, factor_ref, x_vmem, out_vmem, in_sem, out_sem, *, clon, clat, snaps, total_rows):
    load = pltpu.make_async_copy(x_ref, x_vmem, in_sem)
    load.start()
    head, tail = gram_ref[0], gram_ref[1]
    row = lax.broadcasted_iota(jnp.int32, (snaps, snaps), 0)
    col = lax.broadcasted_iota(jnp.int32, (snaps, snaps), 1)
    diagonal = jnp.where(row == col, head, 0.0)
    grow = power_of_two(jnp.sqrt(jnp.sum(diagonal, axis=1, keepdims=True)))
    shrink_rows = jnp.broadcast_to(1.0 / grow, (snaps, snaps))
    shrink_cols = shrink_rows.T
    head = head * shrink_rows * shrink_cols
    tail = tail * shrink_rows * shrink_cols

    upper_one, inverse_one = eliminate(tiles_of(head))

    first, second, third = slices_of(upper_one.T * 128.0)
    a = first.astype(jnp.bfloat16)
    b = second.astype(jnp.bfloat16)
    c = third.astype(jnp.bfloat16)
    exact = dot_nt(a, a)
    mixed = dot_nt(a, b)
    mixed_small = (
        dot_nt(a, c) + dot_nt(b, b) * 0.5 + dot_nt(b, c) * 2.0**-8 + dot_nt(c, c) * 2.0**-17
    )
    mixed = mixed + mixed.T
    mixed_small = mixed_small + mixed_small.T
    missing = (head - exact * 2.0**-14) - mixed * 2.0**-22
    missing = missing - mixed_small * 2.0**-30 + tail
    lower_one = (first + second * 2.0**-8 + third * 2.0**-16) * (1.0 / 128.0)

    near_one = dot_nn(inverse_one, lower_one, HIGHEST)
    left_over = dot_nn(dot_nn(inverse_one, missing, HIGHEST), inverse_one.T, HIGHEST)
    gram_two = dot_nn(near_one, near_one.T, HIGHEST) + left_over
    gram_two = 0.5 * (gram_two + gram_two.T)
    upper_two, inverse_two = eliminate(tiles_of(gram_two))

    scale = float(total_rows) ** 0.5
    factor = dot_nn(upper_two, lower_one.T, HIGHEST) * jnp.broadcast_to(grow, (snaps, snaps)).T
    factor_ref[...] = jnp.where(col >= row, factor * (1.0 / scale), 0.0)

    combined = dot_nn(inverse_two, inverse_one, HIGHEST) * shrink_cols * scale
    load.wait()
    chunk = 8
    copies = []
    for which in range(3):
        for begin in range(0, clon, chunk):
            for lon in range(begin, begin + chunk, 2):
                spot = which * clon + lon
                both = jnp.concatenate([x_vmem[spot], x_vmem[spot + 1]], axis=1)
                value = dot_nn(combined, both, HIGHEST)
                out_vmem[pl.ds(spot, snaps, stride=3 * clon), :] = value[:, :clat]
                out_vmem[pl.ds(spot + 1, snaps, stride=3 * clon), :] = value[:, clat:]
    store = pltpu.make_async_copy(out_vmem, modes_ref, out_sem)
    store.start()
    store.wait()


def orthonormal(gram, x, clon, clat, total_rows):
    snaps = gram.shape[1]
    body = functools.partial(modes_kernel, clon=clon, clat=clat, snaps=snaps, total_rows=total_rows)
    vmem = pl.BlockSpec(memory_space=pltpu.VMEM)
    anywhere = pl.BlockSpec(memory_space=pl.ANY)
    return pl.pallas_call(
        body,
        out_shape=[
            jax.ShapeDtypeStruct((snaps * 3 * clon, clat), jnp.float32),
            jax.ShapeDtypeStruct((snaps, snaps), jnp.float32),
        ],
        in_specs=[vmem, anywhere],
        out_specs=[anywhere, vmem],
        scratch_shapes=[
            pltpu.VMEM((3 * clon, snaps, clat), jnp.float32),
            pltpu.VMEM((snaps * 3 * clon, clat), jnp.float32),
            pltpu.SemaphoreType.DMA,
            pltpu.SemaphoreType.DMA,
        ],
        compiler_params=pltpu.CompilerParams(vmem_limit_bytes=48 * 2**20),
        name="orthonormal",
    )(gram, x)


def add_pairs(left, right):
    total = left[0] + right[0]
    moved = total - left[0]
    lost = (left[0] - (total - moved)) + (right[0] - moved)
    return jnp.stack([total, lost + (left[1] + right[1])])


def summed(pair, count):
    step = 1
    while step < count:
        partners = [(i, i ^ step) for i in range(count)]
        pair = add_pairs(pair, lax.ppermute(pair, BOTH, partners))
        step *= 2
    return pair


def exchange(low, high, west, east, nlon, nlat):
    def move(block, dlon, dlat):
        pairs = []
        for i in range(nlon):
            for j in range(nlat):
                if 0 <= j + dlat < nlat:
                    pairs.append((i * nlat + j, (i + dlon) % nlon * nlat + j + dlat))
        return lax.ppermute(block, BOTH, pairs)

    def swap(block, dlon):
        pairs = [
            (i * nlat + j, (i + dlon) % nlon * nlat + 1 - j) for i in range(nlon) for j in range(2)
        ]
        return lax.ppermute(block, BOTH, pairs)

    from_west = move(east, 1, 0)
    from_east = move(west, -1, 0)
    if nlat == 2:
        position = lax.axis_index("lat")
        edge = jnp.where(position == 0, high, low)
        middle = swap(edge, 0)
        corner_west = swap(edge[-HALO:], 1)
        corner_east = swap(edge[:HALO], -1)
        left = right = (middle, corner_west, corner_east)
    else:
        left = (move(high, 0, 1), move(high[-HALO:], 1, 1), move(high[:HALO], -1, 1))
        right = (move(low, 0, -1), move(low[-HALO:], 1, -1), move(low[:HALO], -1, -1))
    return (from_west, from_east, *left, *right)


def on_device(pressure, ocean_mask):
    snaps, clon, clat = pressure.shape
    nlon, nlat = lax.axis_size("lon"), lax.axis_size("lat")
    turned, west, east, low, high = prepare(pressure, ocean_mask)
    halos = exchange(low, high, west, east, nlon, nlat)
    position = lax.axis_index("lat")
    side = jnp.stack([position, nlat - 1 - position]).astype(jnp.int32)
    x, pair = filtered(side, turned, ocean_mask, halos)
    pair = summed(pair, nlon * nlat)
    total_rows = 3 * clon * clat * nlon * nlat
    modes, factor_r = orthonormal(pair, x, clon, clat, total_rows)
    return modes.reshape(snaps, 3, clon, clat), factor_r


def solution(mesh):
    return jax.shard_map(
        on_device,
        mesh=mesh,
        in_specs=(P(None, "lon", "lat"), P("lon", "lat")),
        out_specs=(P(None, None, "lon", "lat"), P()),
        check_vma=False,
    )
```

```python
import functools

import jax
import jax.numpy as jnp
from jax import lax
from jax.experimental import pallas as pl
from jax.experimental.pallas import tpu as pltpu
from jax.sharding import PartitionSpec as P

PASSES = 4
HALO = PASSES + 1
EDGE = 8
ROUND = 1.5 * 2.0**23
BOTH = ("lon", "lat")
HIGHEST = lax.Precision.HIGHEST
VMEM = pl.BlockSpec(memory_space=pltpu.VMEM)
ANYWHERE = pl.BlockSpec(memory_space=pl.ANY)
PARAMS = pltpu.CompilerParams(vmem_limit_bytes=24 * 2**20)
SMALL = pltpu.CompilerParams(vmem_limit_bytes=12 * 2**20)


def place():
    lat = lax.axis_index("lat")
    return 1 - lax.rem(lax.axis_index("lon"), 2), lat, lat > 0, lat < lax.axis_size("lat") - 1


def f32(*shape):
    return jax.ShapeDtypeStruct(shape, jnp.float32)


def power_of_two(value):
    scaled = value * (2.0**23 + 1.0)
    return scaled - (scaled - value)


def dot_nt(left, right):
    return lax.dot_general(
        left, right, (((1,), (1,)), ((), ())), preferred_element_type=jnp.float32
    )


def dot_nn(left, right, precision=None):
    return lax.dot_general(
        left,
        right,
        (((1,), (0,)), ((), ())),
        precision=precision,
        preferred_element_type=jnp.float32,
    )


def slices_of(scaled):
    first = (scaled + ROUND) - ROUND
    rest = (scaled - first) * 256.0
    second = (rest + ROUND) - ROUND
    rest = (rest - second) * 256.0
    third = (rest + ROUND) - ROUND
    return first, second, third


def longitude(backwards, row, clon):
    return row + backwards * (clon - 1 - 2 * row)


def prepare_kernel(pressure_ref, mask_ref, turned_ref, mask_out_ref, *edge_refs, clon, clat, snaps):
    backwards, lat, _, _ = place()
    line = lax.broadcasted_iota(jnp.int32, (EDGE, clat), 0)
    for row in range(clon):
        spot = longitude(backwards, row, clon)
        plane = pressure_ref[pl.ds(spot, snaps, stride=clon), :].T
        mask = mask_ref[pl.ds(spot, 1), :].astype(jnp.float32)
        turned_ref[row] = plane
        mask_out_ref[row : row + 1] = mask
        low = jnp.where(line < HALO, plane[:EDGE], mask)
        high = jnp.where(line >= EDGE - HALO, plane[clat - EDGE :], mask)
        ends = (low, high) if len(edge_refs) == 2 else (jnp.where(lat == 0, high, low),)
        for edge_ref, end in zip(edge_refs, ends):
            edge_ref[row] = end


def prepare(pressure, mask, edges):
    snaps, clon, clat = pressure.shape
    body = functools.partial(prepare_kernel, clon=clon, clat=clat, snaps=snaps)
    return pl.pallas_call(
        body,
        out_shape=[f32(clon, clat, snaps), f32(clon, clat)]
        + [f32(clon, EDGE, snaps)] * edges,
        in_specs=[VMEM, VMEM],
        compiler_params=SMALL,
        name="prepare",
    )(pressure.reshape(snaps * clon, clat), mask)


def ends_of(left_ref, right_ref, row, has_left, has_right):
    left, right = left_ref[row], right_ref[row]
    return (
        jnp.where(has_left, left, 0.0),
        jnp.where(has_right, right, 0.0),
        jnp.where(has_left, left[:1], 0.0),
        jnp.where(has_right, right[EDGE - 1 :], 0.0),
    )


def pack_kernel(turned_ref, mask_ref, left_ref, right_ref, near_ref, far_ref, *, clon, clat):
    _, _, has_left, has_right = place()
    zeros = jnp.zeros((EDGE - 3, clat), jnp.float32)
    for which, out_ref in enumerate((near_ref, far_ref)):
        for i in range(HALO):
            row = clon - 1 - i if which else i
            left, right, left_mask, right_mask = ends_of(left_ref, right_ref, row, has_left, has_right)
            out_ref[i, :EDGE] = left
            out_ref[i, EDGE : EDGE + clat] = turned_ref[row]
            out_ref[i, EDGE + clat : 2 * EDGE + clat] = right
            out_ref[i, 2 * EDGE + clat :] = jnp.concatenate(
                [mask_ref[row : row + 1], left_mask, right_mask, zeros], axis=0
            )


def pack(turned, mask, left, right):
    clon, clat, snaps = turned.shape
    block = f32(HALO, clat + 3 * EDGE, snaps)
    return pl.pallas_call(
        functools.partial(pack_kernel, clon=clon, clat=clat),
        out_shape=[block, block],
        in_specs=[VMEM] * 4,
        compiler_params=SMALL,
        name="pack",
    )(turned, mask, left, right)


class Tables:
    def __init__(self, masks, keep_lon, keep_lat, quarter):
        self.masks = masks
        self.keep_lon = keep_lon
        self.keep_lat = keep_lat
        self.quarter = quarter

    def put_masks(self, row, own, left, right):
        for which, value in enumerate((own, left, right)):
            self.masks[which, row : row + 1] = value

    def fill(self, rows, clat):
        padded = self.masks.shape[1]
        own, left, right = self.masks[0], self.masks[1], self.masks[2]
        lane = lax.broadcasted_iota(jnp.int32, (padded, clat), 1)
        first_lane = lane == 0
        last_lane = lane == clat - 1

        def up(mask):
            return pltpu.roll(mask, 1, 1)

        def down(mask):
            return pltpu.roll(mask, clat - 1, 1)

        def coefficients(mask, south, north):
            across = pltpu.roll(mask, 1, 0) + pltpu.roll(mask, padded - 1, 0)
            return (
                mask * (1.0 - 0.25 * across),
                mask * (1.0 - 0.25 * (south + north)),
                0.25 * mask,
            )

        middle = coefficients(
            own,
            jnp.where(first_lane, up(left), up(own)),
            jnp.where(last_lane, down(right), down(own)),
        )
        lower = coefficients(left, up(left), jnp.where(last_lane, down(own), down(left)))
        upper = coefficients(right, jnp.where(first_lane, up(own), up(right)), down(right))
        for which, table in enumerate((self.keep_lon, self.keep_lat, self.quarter)):
            column = jnp.concatenate(
                [lower[which].T[clat - EDGE :], middle[which].T, upper[which].T[:EDGE]], axis=0
            )
            for row in rows:
                table[row] = jnp.broadcast_to(
                    column[:, row : row + 1], (clat + 2 * EDGE, table.shape[2])
                )


def sweep(tables, source, target, swept, begin, end, tall):
    lower, upper = EDGE, EDGE + tall

    def one(row, carry):
        around = source[row - 1, lower:upper] + source[row + 1, lower:upper]
        near = tables.quarter[row]
        middle = tables.keep_lon[row] * source[row, lower:upper] + near * around
        swept[row, lower:upper] = middle
        around = swept[row, lower - 1 : upper - 1] + swept[row, lower + 1 : upper + 1]
        target[row, lower:upper] = tables.keep_lat[row] * middle + near * around
        return carry

    lax.fori_loop(begin, end, one, 0)


def clear_ends(swept, rows, tall, snaps):
    zeros = jnp.zeros((EDGE, snaps), jnp.float32)
    for row in rows:
        swept[row, :EDGE] = zeros
        swept[row, EDGE + tall :] = zeros


def fields_of(backwards, tables, source, planes, x_ref, sems, rows, offset, clon, clat, snaps):
    begin = 2 * EDGE
    end = begin + clat
    count = len(rows)
    sign = jnp.where(backwards > 0, -2.0, 2.0)

    def copy(which, i):
        spot = which * count + i
        to = which * clon + longitude(backwards, rows[0] + i, clon)
        return pltpu.make_async_copy(planes.at[spot], x_ref.at[to], sems.at[spot])

    def one(i, top):
        here = rows[0] + i + offset
        center = source[here, begin:end]
        quarter = tables.quarter[here, EDGE : EDGE + clat]
        along_lon = (quarter * sign) * (source[here + 1, begin:end] - source[here - 1, begin:end])
        along_lat = (quarter * 2.0) * (
            source[here, begin + 1 : end + 1] - source[here, begin - 1 : end - 1]
        )
        for which, value in enumerate((center, along_lon, along_lat)):
            value = value.T
            planes[which * count + i] = value
            top = jnp.maximum(top, jnp.abs(value))
        for which in range(3):
            copy(which, i).start()
        return top

    top = lax.fori_loop(0, count, one, jnp.zeros((snaps, clat), jnp.float32))

    def finish():
        def wait(i, carry):
            for which in range(3):
                copy(which, i).wait()
            return carry

        lax.fori_loop(0, count, wait, 0)

    return top, finish


def gram_of(planes, count, top, snaps, clat):
    unit = power_of_two(jnp.maximum(jnp.max(top, axis=1, keepdims=True), 2.0**-60))
    to_whole = jnp.broadcast_to(128.0 / unit, (snaps, clat))
    whole = jnp.zeros((snaps, snaps), jnp.int32)
    first_second = jnp.zeros((snaps, snaps), jnp.float32)
    second_any = jnp.zeros((snaps, 2 * snaps), jnp.float32)
    third_any = jnp.zeros((snaps, 2 * snaps), jnp.float32)
    for begin in range(0, count, 2):
        parts = [slices_of(planes[which] * to_whole) for which in range(begin, min(begin + 2, count))]
        a, b, c = [
            jnp.concatenate([piece.astype(jnp.bfloat16) for piece in same], axis=1) for same in zip(*parts)
        ]
        from_first = dot_nt(a, jnp.concatenate([a, b], axis=0))
        whole = whole + from_first[:, :snaps].astype(jnp.int32)
        first_second = first_second + from_first[:, snaps:]
        second_any = second_any + dot_nt(b, jnp.concatenate([b, c], axis=0))
        third_any = third_any + dot_nt(c, jnp.concatenate([a, c], axis=0))
    fine = (
        first_second
        + (second_any[:, :snaps] * 2.0**-9 + second_any[:, snaps:] * 2.0**-16)
        + (third_any[:, :snaps] * 2.0**-8 + third_any[:, snaps:] * 2.0**-25)
    )
    head = whole.astype(jnp.float32)
    tail = (whole - head.astype(jnp.int32)).astype(jnp.float32) + (fine + fine.T) * 2.0**-8
    total = head + tail
    tail = tail - (total - head)
    unit = jnp.broadcast_to(unit * (1.0 / 128.0), (snaps, snaps))
    return total * unit * unit.T, tail * unit * unit.T


def add_pairs(left, right):
    total = left[0] + right[0]
    moved = total - left[0]
    lost = (left[0] - (total - moved)) + (right[0] - moved)
    return total, lost + (left[1] + right[1])


def put_gram(gram_ref, head, tail):
    half = head.shape[0] // 2
    for core in range(2):
        gram_ref[core, 0] = head[core * half : (core + 1) * half]
        gram_ref[core, 1] = tail[core * half : (core + 1) * half]


def near_kernel(
    turned_ref, mask_ref, left_ref, right_ref, near_ref, x_ref, rim_ref, gram_ref,
    field_a, field_b, swept, masks, keep_lon, keep_lat, quarter, planes, sems, *, clon, clat, snaps,
):
    tall = clat + 2 * EDGE
    lower, upper = EDGE, EDGE + tall
    tables = Tables(masks, keep_lon, keep_lat, quarter)
    wide = clon + HALO
    backwards, _, has_left, has_right = place()
    for i in range(HALO):
        marks = near_ref[i, tall:]
        tables.put_masks(HALO - 1 - i, marks[0:1], marks[1:2], marks[2:3])
    for row in range(clon):
        ends = ends_of(left_ref, right_ref, row, has_left, has_right)
        tables.put_masks(HALO + row, mask_ref[row : row + 1], *ends[2:])
    for row in range(wide, masks.shape[1]):
        zero = jnp.zeros((1, clat), jnp.float32)
        tables.put_masks(row, zero, zero, zero)
    tables.fill(range(wide), clat)
    clear_ends(swept, range(wide), tall, snaps)
    for i in range(HALO):
        row = HALO - 1 - i
        field_a[row, lower:upper] = near_ref[i, :tall] * (quarter[row] * 4.0)

    def start_row(row, carry):
        here = row + HALO
        kept = quarter[here] * 4.0
        left, right, _, _ = ends_of(left_ref, right_ref, row, has_left, has_right)
        field_a[here, lower : lower + EDGE] = left * kept[:EDGE]
        field_a[here, lower + EDGE : upper - EDGE] = turned_ref[row] * kept[EDGE : EDGE + clat]
        field_a[here, upper - EDGE : upper] = right * kept[EDGE + clat :]
        return carry

    lax.fori_loop(0, clon, start_row, 0)
    source, target = field_a, field_b
    for step in range(PASSES + 1):
        rim_ref[step] = source[wide - 2 - step : wide - step, lower:upper]
        if step < PASSES:
            sweep(tables, source, target, swept, step + 1, wide - 1 - step, tall)
            source, target = target, source
    rows = range(clon - HALO)
    top, finish = fields_of(backwards, tables, source, planes, x_ref, sems, rows, HALO, clon, clat, snaps)
    put_gram(gram_ref, *gram_of(planes, 3 * len(rows), top, snaps, clat))
    finish()


def far_kernel(
    mask_ref, left_ref, right_ref, far_ref, rim_ref, gram_in_ref, x_in_ref, x_ref, gram_ref,
    field_a, field_b, swept, masks, keep_lon, keep_lat, quarter, planes, sems, *, clon, clat, snaps,
):
    tall = clat + 2 * EDGE
    lower, upper = EDGE, EDGE + tall
    tables = Tables(masks, keep_lon, keep_lat, quarter)
    backwards, _, has_left, has_right = place()
    skip = clon - HALO - 1
    wide = 2 * HALO + 1
    for row in range(skip, clon):
        ends = ends_of(left_ref, right_ref, row, has_left, has_right)
        tables.put_masks(row - skip, mask_ref[row : row + 1], *ends[2:])
    for i in range(HALO):
        marks = far_ref[i, tall:]
        tables.put_masks(HALO + 1 + i, marks[0:1], marks[1:2], marks[2:3])
    for row in range(wide, masks.shape[1]):
        zero = jnp.zeros((1, clat), jnp.float32)
        tables.put_masks(row, zero, zero, zero)
    tables.fill(range(1, wide), clat)
    clear_ends(swept, range(1, wide - 1), tall, snaps)
    for i in range(HALO):
        row = HALO + 1 + i
        field_a[row, lower:upper] = far_ref[i, :tall] * (quarter[row] * 4.0)
    source, target = field_a, field_b
    for step in range(PASSES + 1):
        source[HALO - 1 - step : HALO + 1 - step, lower:upper] = rim_ref[step]
        if step < PASSES:
            sweep(tables, source, target, swept, HALO - step, 2 * HALO - step, tall)
            source, target = target, source
    rows = range(clon - HALO, clon)
    top, finish = fields_of(backwards, tables, source, planes, x_ref, sems, rows, -skip, clon, clat, snaps)
    gram = gram_of(planes, 3 * len(rows), top, snaps, clat)
    before = [jnp.concatenate([gram_in_ref[0, part], gram_in_ref[1, part]], axis=0) for part in range(2)]
    put_gram(gram_ref, *add_pairs(before, gram))
    finish()


def filter_scratch(wide, planes, clat, snaps):
    tall = clat + 2 * EDGE
    field = pltpu.VMEM((wide, tall + 2 * EDGE, snaps), jnp.float32)
    table = pltpu.VMEM((wide, tall, snaps), jnp.float32)
    masks = pltpu.VMEM((3, -(-wide // 8) * 8, clat), jnp.float32)
    return [
        field, field, field, masks, table, table, table,
        pltpu.VMEM((planes, snaps, clat), jnp.float32),
        pltpu.SemaphoreType.DMA((planes,)),
    ]


def near_part(turned, mask, left, right, near):
    clon, clat, snaps = turned.shape
    planes = 3 * (clon - HALO)
    return pl.pallas_call(
        functools.partial(near_kernel, clon=clon, clat=clat, snaps=snaps),
        out_shape=[
            f32(3 * clon, snaps, clat),
            f32(PASSES + 1, 2, clat + 2 * EDGE, snaps),
            f32(2, 2, snaps // 2, snaps),
        ],
        in_specs=[VMEM] * 5,
        out_specs=[ANYWHERE, VMEM, VMEM],
        scratch_shapes=filter_scratch(clon + HALO, planes, clat, snaps),
        compiler_params=PARAMS,
        cost_estimate=pl.CostEstimate(flops=4_000_000_000, bytes_accessed=8_000_000, transcendentals=0),
        name="near_part",
    )(turned, mask, left, right, near)


def far_part(mask, left, right, far, rim, gram, x, clon, clat, snaps):
    planes = 3 * HALO
    return pl.pallas_call(
        functools.partial(far_kernel, clon=clon, clat=clat, snaps=snaps),
        out_shape=[f32(3 * clon, snaps, clat), f32(2, 2, snaps // 2, snaps)],
        in_specs=[VMEM] * 6 + [ANYWHERE],
        out_specs=[ANYWHERE, VMEM],
        scratch_shapes=filter_scratch(2 * HALO + 1, planes, clat, snaps),
        input_output_aliases={6: 0},
        compiler_params=PARAMS,
        name="far_part",
    )(mask, left, right, far, rim, gram, x)


def spread(row, lane):
    return jnp.broadcast_to(row[:, lane : lane + 1], row.shape)


def eliminate(matrix):
    size = matrix.shape[0]
    count = size // 8
    tiles = [matrix[8 * i : 8 * i + 8, :] for i in range(count)]
    lane = lax.broadcasted_iota(jnp.int32, (8, size), 1)
    sub = lax.broadcasted_iota(jnp.int32, (8, size), 0)
    uppers, inverses = [], []
    for block in range(count):
        base = 8 * block
        panel = tiles[block]
        inside = (lane >= base) & (lane < base + 8)
        rows = [jnp.broadcast_to(panel[r : r + 1, :], (8, size)) for r in range(8)]
        entry = {(r, c): spread(rows[r], base + c) for r in range(8) for c in range(r + 1)}
        units = [jnp.where(lane == base + r, 1.0, 0.0) for r in range(8)]
        factor = {}
        pivots = []
        for k in range(8):
            pivots.append(1.0 / entry[k, k])
            for r in range(k + 1, 8):
                factor[r, k] = entry[r, k] * pivots[k]
            for r in range(k + 1, 8):
                for c in range(k + 1, r + 1):
                    entry[r, c] = entry[r, c] - factor[r, k] * entry[c, k]
        for k in range(8):
            for r in range(k + 1, 8):
                rows[r] = rows[r] - factor[r, k] * rows[k]
                units[r] = units[r] - factor[r, k] * units[k]
        joined = [jnp.where(inside, units[r], rows[r]) for r in range(8)]
        for i in range(block + 1, count):
            raw = [spread(tiles[i], base + k) for k in range(8)]
            tile = jnp.where(inside, 0.0, tiles[i])
            for k in range(8):
                scaled = raw[k] * pivots[k]
                for q in range(k + 1, 8):
                    raw[q] = raw[q] - scaled * entry[q, k]
                tile = tile - scaled * joined[k]
            tiles[i] = tile
        upper = jnp.zeros((8, size), jnp.float32)
        inverse = jnp.zeros((8, size), jnp.float32)
        for r in range(8):
            scale = lax.rsqrt(entry[r, r])
            upper = jnp.where(sub == r, rows[r] * scale, upper)
            inverse = jnp.where(sub == r, joined[r] * scale, inverse)
        uppers.append(jnp.where(lane >= base + sub, upper, 0.0))
        inverses.append(jnp.where(lane <= base + sub, inverse, 0.0))
    return jnp.concatenate(uppers, axis=0), jnp.concatenate(inverses, axis=0)


def thirds(value):
    first = value.astype(jnp.bfloat16)
    rest = value - first.astype(jnp.float32)
    second = rest.astype(jnp.bfloat16)
    third = (rest - second.astype(jnp.float32)).astype(jnp.bfloat16)
    return first, second, third


def modes_kernel(gram_ref, x_ref, modes_ref, factor_ref, x_vmem, out_vmem, in_sem, out_sems, *, clon, clat, snaps, total_rows):
    load = pltpu.make_async_copy(x_ref, x_vmem, in_sem)
    load.start()
    head, tail = [jnp.concatenate([gram_ref[0, part], gram_ref[1, part]], axis=0) for part in range(2)]
    row = lax.broadcasted_iota(jnp.int32, (snaps, snaps), 0)
    col = lax.broadcasted_iota(jnp.int32, (snaps, snaps), 1)
    diagonal = jnp.where(row == col, head, 0.0)
    grow = power_of_two(jnp.sqrt(jnp.sum(diagonal, axis=1, keepdims=True)))
    shrink_rows = jnp.broadcast_to(1.0 / grow, (snaps, snaps))
    shrink_cols = shrink_rows.T
    head = head * shrink_rows * shrink_cols
    tail = tail * shrink_rows * shrink_cols

    upper_one, inverse_one = eliminate(head)

    first, second, third = slices_of(upper_one.T * 128.0)
    a = first.astype(jnp.bfloat16)
    b = second.astype(jnp.bfloat16)
    c = third.astype(jnp.bfloat16)
    exact = dot_nt(a, a)
    mixed = dot_nt(a, b)
    mixed_small = (
        dot_nt(a, c) + dot_nt(b, b) * 0.5 + dot_nt(b, c) * 2.0**-8 + dot_nt(c, c) * 2.0**-17
    )
    mixed = mixed + mixed.T
    mixed_small = mixed_small + mixed_small.T
    missing = (head - exact * 2.0**-14) - mixed * 2.0**-22
    missing = missing - mixed_small * 2.0**-30 + tail
    lower_one = (first + second * 2.0**-8 + third * 2.0**-16) * (1.0 / 128.0)

    near_one = dot_nn(inverse_one, lower_one, HIGHEST)
    left_over = dot_nn(dot_nn(inverse_one, missing, HIGHEST), inverse_one.T, HIGHEST)
    gram_two = dot_nn(near_one, near_one.T, HIGHEST) + left_over
    gram_two = 0.5 * (gram_two + gram_two.T)
    upper_two, inverse_two = eliminate(gram_two)

    scale = float(total_rows) ** 0.5
    combined = dot_nn(inverse_two, inverse_one, HIGHEST) * shrink_cols * scale
    first, second, third = thirds(combined)
    first_second = jnp.concatenate([first, second], axis=1)
    first_third = jnp.concatenate([first, third], axis=1)
    load.wait()
    copies = []
    for which in range(3):
        for part in range(clon // 8):
            spot = which * (clon // 8) + part
            flat = out_vmem.at[spot].reshape(snaps * 8, clat)
            for lon in range(0, 8, 2):
                plane = which * clon + part * 8 + lon
                x_one, x_two, x_three = thirds(jnp.concatenate([x_vmem[plane], x_vmem[plane + 1]], axis=1))
                value = (
                    dot_nn(first_third, jnp.concatenate([x_three, x_one], axis=0))
                    + dot_nn(first_second, jnp.concatenate([x_two, x_two], axis=0))
                ) + dot_nn(first_second, jnp.concatenate([x_one, x_one], axis=0))
                flat[pl.ds(lon, snaps, stride=8), :] = value[:, :clat]
                flat[pl.ds(lon + 1, snaps, stride=8), :] = value[:, clat:]
            copy = pltpu.make_async_copy(
                out_vmem.at[spot], modes_ref.at[:, which, pl.ds(part * 8, 8), :], out_sems.at[spot]
            )
            copy.start()
            copies.append(copy)
    factor = dot_nn(upper_two, lower_one.T, HIGHEST) * jnp.broadcast_to(grow, (snaps, snaps)).T
    factor_ref[...] = jnp.where(col >= row, factor * (1.0 / scale), 0.0)
    for copy in copies:
        copy.wait()


def orthonormal(gram, x, clon, clat, total_rows):
    snaps = gram.shape[3]
    parts = 3 * clon // 8
    return pl.pallas_call(
        functools.partial(modes_kernel, clon=clon, clat=clat, snaps=snaps, total_rows=total_rows),
        out_shape=[f32(snaps, 3, clon, clat), f32(snaps, snaps)],
        in_specs=[VMEM, ANYWHERE],
        out_specs=[ANYWHERE, VMEM],
        scratch_shapes=[
            pltpu.VMEM((3 * clon, snaps, clat), jnp.float32),
            pltpu.VMEM((parts, snaps, 8, clat), jnp.float32),
            pltpu.SemaphoreType.DMA,
            pltpu.SemaphoreType.DMA((parts,)),
        ],
        compiler_params=PARAMS,
        name="orthonormal",
    )(gram, x)


def summed(halves, nlon, nlat):
    count = nlon * nlat
    core = lax.axis_index("lon") % 2

    def partner(value, step):
        return lax.ppermute(value, BOTH, [(i, i ^ step) for i in range(count)])

    def add(left, right):
        return jnp.stack(add_pairs(left, right))

    mine = add(
        jnp.where(core == 0, halves[0], halves[1]),
        partner(jnp.where(core == 0, halves[1], halves[0]), nlat),
    )
    steps = [1 << bit for bit in range(count.bit_length() - 1) if 1 << bit != nlat]
    while steps:
        if len(steps) >= 2:
            low, high = steps[0], steps[1]
            others = [partner(mine, step) for step in (low, high, low ^ high)]
            mine = add(add(mine, others[0]), add(others[1], others[2]))
            steps = steps[2:]
        else:
            mine = add(mine, partner(mine, steps[0]))
            steps = steps[1:]
    other = partner(mine, nlat)
    return jnp.where(core == 0, jnp.stack([mine, other]), jnp.stack([other, mine]))


def on_device(pressure, ocean_mask):
    snaps, clon, clat = pressure.shape
    nlon, nlat = lax.axis_size("lon"), lax.axis_size("lat")
    merged = nlat == 2
    turned, mask, *edges = prepare(pressure, ocean_mask, 1 if merged else 2)
    if merged:
        left = right = lax.ppermute(edges[0], "lat", [(0, 1), (1, 0)])
    else:
        left = lax.ppermute(edges[1], "lat", [(i, i + 1) for i in range(nlat - 1)])
        right = lax.ppermute(edges[0], "lat", [(i + 1, i) for i in range(nlat - 1)])
    near, far = pack(turned, mask, left, right)
    far = lax.ppermute(
        far, "lon", [(i, (i + 1 if i % 2 else i - 1) % nlon) for i in range(nlon)]
    )
    near = lax.ppermute(near, "lon", [(i, i ^ 1) for i in range(nlon)])
    x, rim, gram = near_part(turned, mask, left, right, near)
    x, gram = far_part(mask, left, right, far, rim, gram, x, clon, clat, snaps)
    gram = summed(gram, nlon, nlat)
    return tuple(orthonormal(gram, x, clon, clat, 3 * clon * clat * nlon * nlat))


def solution(mesh):
    return jax.shard_map(
        on_device,
        mesh=mesh,
        in_specs=(P(None, "lon", "lat"), P("lon", "lat")),
        out_specs=(P(None, None, "lon", "lat"), P()),
        check_vma=False,
    )
```

```python
import functools

import jax
import jax.numpy as jnp
from jax import lax
from jax.experimental import pallas as pl
from jax.experimental.pallas import tpu as pltpu
from jax.sharding import PartitionSpec as P

PASSES = 4
HALO = PASSES + 1
EDGE = 8
NEAR_ONE = 2.0**-6
ROUND = 1.5 * 2.0**23
BOTH = ("lon", "lat")
HIGHEST = lax.Precision.HIGHEST
VMEM = pl.BlockSpec(memory_space=pltpu.VMEM)
ANYWHERE = pl.BlockSpec(memory_space=pl.ANY)
PARAMS = pltpu.CompilerParams(vmem_limit_bytes=24 * 2**20)
SMALL = pltpu.CompilerParams(vmem_limit_bytes=12 * 2**20)


def place():
    lat = lax.axis_index("lat")
    return 1 - lax.rem(lax.axis_index("lon"), 2), lat, lat > 0, lat < lax.axis_size("lat") - 1


def f32(*shape):
    return jax.ShapeDtypeStruct(shape, jnp.float32)


def power_of_two(value):
    scaled = value * (2.0**23 + 1.0)
    return scaled - (scaled - value)


def dot_nt(left, right):
    return lax.dot_general(
        left, right, (((1,), (1,)), ((), ())), preferred_element_type=jnp.float32
    )


def dot_nn(left, right, precision=None):
    return lax.dot_general(
        left,
        right,
        (((1,), (0,)), ((), ())),
        precision=precision,
        preferred_element_type=jnp.float32,
    )


def slices_of(scaled):
    first = (scaled + ROUND) - ROUND
    rest = (scaled - first) * 256.0
    second = (rest + ROUND) - ROUND
    rest = (rest - second) * 256.0
    third = (rest + ROUND) - ROUND
    return first, second, third


def longitude(backwards, row, clon):
    return row + backwards * (clon - 1 - 2 * row)


def prepare_kernel(pressure_ref, mask_ref, turned_ref, mask_out_ref, *edge_refs, clon, clat, snaps):
    backwards, lat, _, _ = place()
    line = lax.broadcasted_iota(jnp.int32, (EDGE, clat), 0)
    for row in range(clon):
        spot = longitude(backwards, row, clon)
        plane = pressure_ref[pl.ds(spot, snaps, stride=clon), :].T
        mask = mask_ref[pl.ds(spot, 1), :]
        turned_ref[row] = plane
        mask_out_ref[row : row + 1] = mask
        low = jnp.where(line < HALO, plane[:EDGE], mask)
        high = jnp.where(line >= EDGE - HALO, plane[clat - EDGE :], mask)
        ends = (low, high) if len(edge_refs) == 2 else (jnp.where(lat == 0, high, low),)
        for edge_ref, end in zip(edge_refs, ends):
            edge_ref[row] = end


def prepare(pressure, mask, edges):
    snaps, clon, clat = pressure.shape
    body = functools.partial(prepare_kernel, clon=clon, clat=clat, snaps=snaps)
    return pl.pallas_call(
        body,
        out_shape=[f32(clon, clat, snaps), f32(clon, clat)]
        + [f32(clon, EDGE, snaps)] * edges,
        in_specs=[VMEM, VMEM],
        compiler_params=SMALL,
        name="prepare",
    )(pressure.reshape(snaps * clon, clat), mask)


def ends_of(left_ref, right_ref, row, has_left, has_right):
    left, right = left_ref[row], right_ref[row]
    return (
        jnp.where(has_left, left, 0.0),
        jnp.where(has_right, right, 0.0),
        jnp.where(has_left, left[:1], 0.0),
        jnp.where(has_right, right[EDGE - 1 :], 0.0),
    )


def pack_kernel(turned_ref, mask_ref, left_ref, right_ref, near_ref, far_ref, *, clon, clat):
    _, _, has_left, has_right = place()
    zeros = jnp.zeros((EDGE - 3, clat), jnp.float32)
    for which, out_ref in enumerate((near_ref, far_ref)):
        for i in range(HALO):
            row = clon - 1 - i if which else i
            left, right, left_mask, right_mask = ends_of(left_ref, right_ref, row, has_left, has_right)
            out_ref[i, :EDGE] = left
            out_ref[i, EDGE : EDGE + clat] = turned_ref[row]
            out_ref[i, EDGE + clat : 2 * EDGE + clat] = right
            out_ref[i, 2 * EDGE + clat :] = jnp.concatenate(
                [mask_ref[row : row + 1], left_mask, right_mask, zeros], axis=0
            )


def pack(turned, mask, left, right):
    clon, clat, snaps = turned.shape
    block = f32(HALO, clat + 3 * EDGE, snaps)
    return pl.pallas_call(
        functools.partial(pack_kernel, clon=clon, clat=clat),
        out_shape=[block, block],
        in_specs=[VMEM] * 4,
        compiler_params=SMALL,
        name="pack",
    )(turned, mask, left, right)


class Tables:
    def __init__(self, masks, keep_lon, keep_lat, quarter):
        self.masks = masks
        self.keep_lon = keep_lon
        self.keep_lat = keep_lat
        self.quarter = quarter

    def put_masks(self, row, own, left, right):
        for which, value in enumerate((own, left, right)):
            self.masks[which, row : row + 1] = value

    def fill(self, rows, clat):
        padded = self.masks.shape[1]
        own, left, right = self.masks[0], self.masks[1], self.masks[2]
        lane = lax.broadcasted_iota(jnp.int32, (padded, clat), 1)
        first_lane = lane == 0
        last_lane = lane == clat - 1

        def up(mask):
            return pltpu.roll(mask, 1, 1)

        def down(mask):
            return pltpu.roll(mask, clat - 1, 1)

        def coefficients(mask, south, north):
            across = pltpu.roll(mask, 1, 0) + pltpu.roll(mask, padded - 1, 0)
            return (
                mask * (1.0 - 0.25 * across),
                mask * (1.0 - 0.25 * (south + north)),
                0.25 * mask,
            )

        middle = coefficients(
            own,
            jnp.where(first_lane, up(left), up(own)),
            jnp.where(last_lane, down(right), down(own)),
        )
        lower = coefficients(left, up(left), jnp.where(last_lane, down(own), down(left)))
        upper = coefficients(right, jnp.where(first_lane, up(own), up(right)), down(right))
        for which, table in enumerate((self.keep_lon, self.keep_lat, self.quarter)):
            column = jnp.concatenate(
                [lower[which].T[clat - EDGE :], middle[which].T, upper[which].T[:EDGE]], axis=0
            )
            for row in rows:
                table[row] = jnp.broadcast_to(
                    column[:, row : row + 1], (clat + 2 * EDGE, table.shape[2])
                )


def sweep(tables, source, target, swept, begin, end, tall):
    lower, upper = EDGE, EDGE + tall

    def one(row, carry):
        around = source[row - 1, lower:upper] + source[row + 1, lower:upper]
        near = tables.quarter[row]
        middle = tables.keep_lon[row] * source[row, lower:upper] + near * around
        swept[row, lower:upper] = middle
        around = swept[row, lower - 1 : upper - 1] + swept[row, lower + 1 : upper + 1]
        target[row, lower:upper] = tables.keep_lat[row] * middle + near * around
        return carry

    lax.fori_loop(begin, end, one, 0)


def clear_ends(swept, rows, tall, snaps):
    zeros = jnp.zeros((EDGE, snaps), jnp.float32)
    for row in rows:
        swept[row, :EDGE] = zeros
        swept[row, EDGE + tall :] = zeros


def fields_of(backwards, tables, source, planes, rows, offset, clat, snaps):
    begin = 2 * EDGE
    end = begin + clat
    count = len(rows)
    sign = jnp.where(backwards > 0, -2.0, 2.0)

    def one(i, top):
        here = rows[0] + i + offset
        center = source[here, begin:end]
        quarter = tables.quarter[here, EDGE : EDGE + clat]
        along_lon = (quarter * sign) * (source[here + 1, begin:end] - source[here - 1, begin:end])
        along_lat = (quarter * 2.0) * (
            source[here, begin + 1 : end + 1] - source[here, begin - 1 : end - 1]
        )
        for which, value in enumerate((center, along_lon, along_lat)):
            value = value.T
            planes[which * count + i] = value
            top = jnp.maximum(top, jnp.abs(value))
        return top

    return lax.fori_loop(0, count, one, jnp.zeros((snaps, clat), jnp.float32))


def gram_of(planes, count, top, snaps, clat):
    unit = power_of_two(jnp.maximum(jnp.max(top, axis=1, keepdims=True), 2.0**-60))
    to_whole = jnp.broadcast_to(128.0 / unit, (snaps, clat))
    whole = jnp.zeros((snaps, snaps), jnp.int32)
    first_second = jnp.zeros((snaps, snaps), jnp.float32)
    second_any = jnp.zeros((snaps, 2 * snaps), jnp.float32)
    third_any = jnp.zeros((snaps, 2 * snaps), jnp.float32)
    for begin in range(0, count, 2):
        parts = [slices_of(planes[which] * to_whole) for which in range(begin, min(begin + 2, count))]
        a, b, c = [
            jnp.concatenate([piece.astype(jnp.bfloat16) for piece in same], axis=1) for same in zip(*parts)
        ]
        from_first = dot_nt(a, jnp.concatenate([a, b], axis=0))
        whole = whole + from_first[:, :snaps].astype(jnp.int32)
        first_second = first_second + from_first[:, snaps:]
        second_any = second_any + dot_nt(b, jnp.concatenate([b, c], axis=0))
        third_any = third_any + dot_nt(c, jnp.concatenate([a, c], axis=0))
    fine = (
        first_second
        + (second_any[:, :snaps] * 2.0**-9 + second_any[:, snaps:] * 2.0**-16)
        + (third_any[:, :snaps] * 2.0**-8 + third_any[:, snaps:] * 2.0**-25)
    )
    head = whole.astype(jnp.float32)
    tail = (whole - head.astype(jnp.int32)).astype(jnp.float32) + (fine + fine.T) * 2.0**-8
    total = head + tail
    tail = tail - (total - head)
    unit = jnp.broadcast_to(unit * (1.0 / 128.0), (snaps, snaps))
    return total * unit * unit.T, tail * unit * unit.T


def add_pairs(left, right):
    total = left[0] + right[0]
    moved = total - left[0]
    lost = (left[0] - (total - moved)) + (right[0] - moved)
    return total, lost + (left[1] + right[1])


def put_gram(gram_ref, head, tail):
    half = head.shape[0] // 2
    for core in range(2):
        gram_ref[core, 0] = head[core * half : (core + 1) * half]
        gram_ref[core, 1] = tail[core * half : (core + 1) * half]


def near_kernel(
    turned_ref, mask_ref, left_ref, right_ref, near_ref, x_ref, rim_ref, gram_ref,
    field_a, field_b, swept, masks, keep_lon, keep_lat, quarter, *, clon, clat, snaps,
):
    tall = clat + 2 * EDGE
    lower, upper = EDGE, EDGE + tall
    tables = Tables(masks, keep_lon, keep_lat, quarter)
    wide = clon + HALO
    backwards, _, has_left, has_right = place()
    for i in range(HALO):
        marks = near_ref[i, tall:]
        tables.put_masks(HALO - 1 - i, marks[0:1], marks[1:2], marks[2:3])
    for row in range(clon):
        ends = ends_of(left_ref, right_ref, row, has_left, has_right)
        tables.put_masks(HALO + row, mask_ref[row : row + 1], *ends[2:])
    for row in range(wide, masks.shape[1]):
        zero = jnp.zeros((1, clat), jnp.float32)
        tables.put_masks(row, zero, zero, zero)
    tables.fill(range(wide), clat)
    clear_ends(swept, range(wide), tall, snaps)
    for i in range(HALO):
        row = HALO - 1 - i
        field_a[row, lower:upper] = near_ref[i, :tall] * (quarter[row] * 4.0)

    def start_row(row, carry):
        here = row + HALO
        kept = quarter[here] * 4.0
        left, right, _, _ = ends_of(left_ref, right_ref, row, has_left, has_right)
        field_a[here, lower : lower + EDGE] = left * kept[:EDGE]
        field_a[here, lower + EDGE : upper - EDGE] = turned_ref[row] * kept[EDGE : EDGE + clat]
        field_a[here, upper - EDGE : upper] = right * kept[EDGE + clat :]
        return carry

    lax.fori_loop(0, clon, start_row, 0)
    source, target = field_a, field_b
    for step in range(PASSES + 1):
        rim_ref[step] = source[wide - 2 - step : wide - step, lower:upper]
        if step < PASSES:
            sweep(tables, source, target, swept, step + 1, wide - 1 - step, tall)
            source, target = target, source
    rows = range(clon - HALO)
    top = fields_of(backwards, tables, source, x_ref, rows, HALO, clat, snaps)
    put_gram(gram_ref, *gram_of(x_ref, 3 * len(rows), top, snaps, clat))


def far_kernel(
    mask_ref, left_ref, right_ref, far_ref, rim_ref, gram_in_ref, x_ref, gram_ref,
    field_a, field_b, swept, masks, keep_lon, keep_lat, quarter, *, clon, clat, snaps,
):
    tall = clat + 2 * EDGE
    lower, upper = EDGE, EDGE + tall
    tables = Tables(masks, keep_lon, keep_lat, quarter)
    backwards, _, has_left, has_right = place()
    skip = clon - HALO - 1
    wide = 2 * HALO + 1
    for row in range(skip, clon):
        ends = ends_of(left_ref, right_ref, row, has_left, has_right)
        tables.put_masks(row - skip, mask_ref[row : row + 1], *ends[2:])
    for i in range(HALO):
        marks = far_ref[i, tall:]
        tables.put_masks(HALO + 1 + i, marks[0:1], marks[1:2], marks[2:3])
    for row in range(wide, masks.shape[1]):
        zero = jnp.zeros((1, clat), jnp.float32)
        tables.put_masks(row, zero, zero, zero)
    tables.fill(range(1, wide), clat)
    clear_ends(swept, range(1, wide - 1), tall, snaps)
    for i in range(HALO):
        row = HALO + 1 + i
        field_a[row, lower:upper] = far_ref[i, :tall] * (quarter[row] * 4.0)
    source, target = field_a, field_b
    for step in range(PASSES + 1):
        source[HALO - 1 - step : HALO + 1 - step, lower:upper] = rim_ref[step]
        if step < PASSES:
            sweep(tables, source, target, swept, HALO - step, 2 * HALO - step, tall)
            source, target = target, source
    rows = range(clon - HALO, clon)
    top = fields_of(backwards, tables, source, x_ref, rows, -skip, clat, snaps)
    gram = gram_of(x_ref, 3 * len(rows), top, snaps, clat)
    before = [jnp.concatenate([gram_in_ref[0, part], gram_in_ref[1, part]], axis=0) for part in range(2)]
    put_gram(gram_ref, *add_pairs(before, gram))


def filter_scratch(wide, clat, snaps):
    tall = clat + 2 * EDGE
    field = pltpu.VMEM((wide, tall + 2 * EDGE, snaps), jnp.float32)
    table = pltpu.VMEM((wide, tall, snaps), jnp.float32)
    masks = pltpu.VMEM((3, -(-wide // 8) * 8, clat), jnp.float32)
    return [field, field, field, masks, table, table, table]


def near_part(turned, mask, left, right, near):
    clon, clat, snaps = turned.shape
    return pl.pallas_call(
        functools.partial(near_kernel, clon=clon, clat=clat, snaps=snaps),
        out_shape=[
            f32(3 * (clon - HALO), snaps, clat),
            f32(PASSES + 1, 2, clat + 2 * EDGE, snaps),
            f32(2, 2, snaps // 2, snaps),
        ],
        in_specs=[VMEM] * 5,
        out_specs=[VMEM, VMEM, VMEM],
        scratch_shapes=filter_scratch(clon + HALO, clat, snaps),
        compiler_params=PARAMS,
        cost_estimate=pl.CostEstimate(flops=4_000_000_000, bytes_accessed=8_000_000, transcendentals=0),
        name="near_part",
    )(turned, mask, left, right, near)


def far_part(mask, left, right, far, rim, gram, clon, clat, snaps):
    return pl.pallas_call(
        functools.partial(far_kernel, clon=clon, clat=clat, snaps=snaps),
        out_shape=[f32(3 * HALO, snaps, clat), f32(2, 2, snaps // 2, snaps)],
        in_specs=[VMEM] * 6,
        out_specs=[VMEM, VMEM],
        scratch_shapes=filter_scratch(2 * HALO + 1, clat, snaps),
        compiler_params=PARAMS,
        name="far_part",
    )(mask, left, right, far, rim, gram)


def spread(row, lane):
    return jnp.broadcast_to(row[:, lane : lane + 1], row.shape)


def eliminate(matrix):
    size = matrix.shape[0]
    count = size // 8
    tiles = [matrix[8 * i : 8 * i + 8, :] for i in range(count)]
    lane = lax.broadcasted_iota(jnp.int32, (8, size), 1)
    sub = lax.broadcasted_iota(jnp.int32, (8, size), 0)
    uppers, inverses = [], []
    for block in range(count):
        base = 8 * block
        panel = tiles[block]
        inside = (lane >= base) & (lane < base + 8)
        rows = [jnp.broadcast_to(panel[r : r + 1, :], (8, size)) for r in range(8)]
        entry = {(r, c): spread(rows[r], base + c) for r in range(8) for c in range(r + 1)}
        units = [jnp.where(lane == base + r, 1.0, 0.0) for r in range(8)]
        factor = {}
        pivots = []
        for k in range(8):
            pivots.append(1.0 / entry[k, k])
            for r in range(k + 1, 8):
                factor[r, k] = entry[r, k] * pivots[k]
            for r in range(k + 1, 8):
                for c in range(k + 1, r + 1):
                    entry[r, c] = entry[r, c] - factor[r, k] * entry[c, k]
        for k in range(8):
            for r in range(k + 1, 8):
                rows[r] = rows[r] - factor[r, k] * rows[k]
                units[r] = units[r] - factor[r, k] * units[k]
        joined = [jnp.where(inside, units[r], rows[r]) for r in range(8)]
        for i in range(block + 1, count):
            raw = [spread(tiles[i], base + k) for k in range(8)]
            tile = jnp.where(inside, 0.0, tiles[i])
            for k in range(8):
                scaled = raw[k] * pivots[k]
                for q in range(k + 1, 8):
                    raw[q] = raw[q] - scaled * entry[q, k]
                tile = tile - scaled * joined[k]
            tiles[i] = tile
        upper = jnp.zeros((8, size), jnp.float32)
        inverse = jnp.zeros((8, size), jnp.float32)
        for r in range(8):
            scale = lax.rsqrt(entry[r, r])
            upper = jnp.where(sub == r, rows[r] * scale, upper)
            inverse = jnp.where(sub == r, joined[r] * scale, inverse)
        uppers.append(jnp.where(lane >= base + sub, upper, 0.0))
        inverses.append(jnp.where(lane <= base + sub, inverse, 0.0))
    return jnp.concatenate(uppers, axis=0), jnp.concatenate(inverses, axis=0)


def thirds(value):
    first = value.astype(jnp.bfloat16)
    rest = value - first.astype(jnp.float32)
    second = rest.astype(jnp.bfloat16)
    third = (rest - second.astype(jnp.float32)).astype(jnp.bfloat16)
    return first, second, third


def modes_kernel(
    gram_ref, near_ref, far_ref, modes_ref, factor_ref, out_vmem, upper_vmem, combined_vmem, out_sems, *, clon, clat, snaps, total_rows
):
    head, tail = [jnp.concatenate([gram_ref[0, part], gram_ref[1, part]], axis=0) for part in range(2)]
    row = lax.broadcasted_iota(jnp.int32, (snaps, snaps), 0)
    col = lax.broadcasted_iota(jnp.int32, (snaps, snaps), 1)
    diagonal = jnp.where(row == col, head, 0.0)
    grow = power_of_two(jnp.sqrt(jnp.sum(diagonal, axis=1, keepdims=True)))
    shrink_rows = jnp.broadcast_to(1.0 / grow, (snaps, snaps))
    shrink_cols = shrink_rows.T
    head = head * shrink_rows * shrink_cols
    tail = tail * shrink_rows * shrink_cols

    upper_one, inverse_one = eliminate(head)

    first, second, third = slices_of(upper_one.T * 128.0)
    a = first.astype(jnp.bfloat16)
    b = second.astype(jnp.bfloat16)
    c = third.astype(jnp.bfloat16)
    exact = dot_nt(a, a)
    mixed = dot_nt(a, b)
    mixed_small = (
        dot_nt(a, c) + dot_nt(b, b) * 0.5 + dot_nt(b, c) * 2.0**-8 + dot_nt(c, c) * 2.0**-17
    )
    mixed = mixed + mixed.T
    mixed_small = mixed_small + mixed_small.T
    missing = (head - exact * 2.0**-14) - mixed * 2.0**-22
    missing = missing - mixed_small * 2.0**-30 + tail
    lower_one = (first + second * 2.0**-8 + third * 2.0**-16) * (1.0 / 128.0)

    near_one = dot_nn(inverse_one, lower_one, HIGHEST)
    left_over = dot_nn(dot_nn(inverse_one, missing, HIGHEST), inverse_one.T, HIGHEST)
    gram_two = dot_nn(near_one, near_one.T, HIGHEST) + left_over
    gram_two = 0.5 * (gram_two + gram_two.T)
    difference = gram_two - jnp.where(row == col, 1.0, 0.0)

    def lower_half(matrix):
        return jnp.where(row > col, matrix, jnp.where(row == col, 0.5 * matrix, 0.0))

    small = jnp.sum(difference * difference) < NEAR_ONE**2

    @pl.when(small)
    def _():
        k = lower_half(difference)
        for _ in range(2):
            rough = k.astype(jnp.bfloat16)
            k = lower_half(difference - dot_nt(rough, rough))
        rough = k.astype(jnp.bfloat16)
        square = dot_nn(rough, rough)
        change = k - dot_nn(rough, (k - square).astype(jnp.bfloat16))
        upper_vmem[...] = k.T + jnp.where(row == col, 1.0, 0.0)
        combined_vmem[...] = inverse_one - dot_nn(change, inverse_one, HIGHEST)

    @pl.when(jnp.logical_not(small))
    def _():
        upper, inverse = eliminate(gram_two)
        upper_vmem[...] = upper
        combined_vmem[...] = dot_nn(inverse, inverse_one, HIGHEST)

    scale = float(total_rows) ** 0.5
    combined = combined_vmem[...] * shrink_cols * scale
    first, second, third = thirds(combined)
    first_second = jnp.concatenate([first, second], axis=1)
    first_third = jnp.concatenate([first, third], axis=1)
    backwards, _, _, _ = place()
    near_rows = clon - HALO

    def plane(which, q):
        if q < near_rows:
            return near_ref[which * near_rows + q]
        return far_ref[which * HALO + q - near_rows]

    copies = []
    for which in range(3):
        for part in range(clon // 8):
            spot = which * (clon // 8) + part
            flat = out_vmem.at[spot].reshape(snaps * 8, clat)
            for lon in range(0, 8, 2):
                q = part * 8 + lon
                both = jnp.concatenate([plane(which, q), plane(which, q + 1)], axis=1)
                x_one, x_two, x_three = thirds(both)
                value = (
                    dot_nn(first_third, jnp.concatenate([x_three, x_one], axis=0))
                    + dot_nn(first_second, jnp.concatenate([x_two, x_two], axis=0))
                ) + dot_nn(first_second, jnp.concatenate([x_one, x_one], axis=0))
                for side in range(2):
                    to = longitude(backwards, lon + side, 8)
                    flat[pl.ds(to, snaps, stride=8), :] = value[:, side * clat : (side + 1) * clat]
            to = pl.multiple_of(8 * longitude(backwards, part, clon // 8), 8)
            copy = pltpu.make_async_copy(
                out_vmem.at[spot], modes_ref.at[:, which, pl.ds(to, 8), :], out_sems.at[spot]
            )
            copy.start()
            copies.append(copy)
    factor = dot_nn(upper_vmem[...], lower_one.T, HIGHEST) * jnp.broadcast_to(grow, (snaps, snaps)).T
    factor_ref[...] = jnp.where(col >= row, factor * (1.0 / scale), 0.0)
    for copy in copies:
        copy.wait()


def orthonormal(gram, x_near, x_far, clon, clat, total_rows):
    snaps = gram.shape[3]
    parts = 3 * clon // 8
    return pl.pallas_call(
        functools.partial(modes_kernel, clon=clon, clat=clat, snaps=snaps, total_rows=total_rows),
        out_shape=[f32(snaps, 3, clon, clat), f32(snaps, snaps)],
        in_specs=[VMEM] * 3,
        out_specs=[ANYWHERE, VMEM],
        scratch_shapes=[
            pltpu.VMEM((parts, snaps, 8, clat), jnp.float32),
            pltpu.VMEM((snaps, snaps), jnp.float32),
            pltpu.VMEM((snaps, snaps), jnp.float32),
            pltpu.SemaphoreType.DMA((parts,)),
        ],
        compiler_params=PARAMS,
        name="orthonormal",
    )(gram, x_near, x_far)


def summed(halves, nlon, nlat):
    count = nlon * nlat
    core = lax.axis_index("lon") % 2

    def partner(value, step):
        return lax.ppermute(value, BOTH, [(i, i ^ step) for i in range(count)])

    def add(left, right):
        return jnp.stack(add_pairs(left, right))

    mine = add(
        jnp.where(core == 0, halves[0], halves[1]),
        partner(jnp.where(core == 0, halves[1], halves[0]), nlat),
    )
    steps = [1 << bit for bit in range(count.bit_length() - 1) if 1 << bit != nlat]
    while steps:
        if len(steps) >= 2:
            low, high = steps[0], steps[1]
            others = [partner(mine, step) for step in (low, high, low ^ high)]
            mine = add(add(mine, others[0]), add(others[1], others[2]))
            steps = steps[2:]
        else:
            mine = add(mine, partner(mine, steps[0]))
            steps = steps[1:]
    other = partner(mine, nlat)
    return jnp.where(core == 0, jnp.stack([mine, other]), jnp.stack([other, mine]))


def on_device(pressure, ocean_mask):
    snaps, clon, clat = pressure.shape
    nlon, nlat = lax.axis_size("lon"), lax.axis_size("lat")
    merged = nlat == 2
    turned, mask, *edges = prepare(pressure, ocean_mask.astype(jnp.float32), 1 if merged else 2)
    if merged:
        left = right = lax.ppermute(edges[0], "lat", [(0, 1), (1, 0)])
    else:
        left = lax.ppermute(edges[1], "lat", [(i, i + 1) for i in range(nlat - 1)])
        right = lax.ppermute(edges[0], "lat", [(i + 1, i) for i in range(nlat - 1)])
    near, far = pack(turned, mask, left, right)
    far = lax.ppermute(
        far, "lon", [(i, (i + 1 if i % 2 else i - 1) % nlon) for i in range(nlon)]
    )
    near = lax.ppermute(near, "lon", [(i, i ^ 1) for i in range(nlon)])
    x_near, rim, gram = near_part(turned, mask, left, right, near)
    x_far, gram = far_part(mask, left, right, far, rim, gram, clon, clat, snaps)
    gram = summed(gram, nlon, nlat)
    return tuple(orthonormal(gram, x_near, x_far, clon, clat, 3 * clon * clat * nlon * nlat))


def solution(mesh):
    return jax.shard_map(
        on_device,
        mesh=mesh,
        in_specs=(P(None, "lon", "lat"), P("lon", "lat")),
        out_specs=(P(None, None, "lon", "lat"), P()),
        check_vma=False,
    )
```

```python
import functools

import jax
import jax.numpy as jnp
from jax import lax
from jax.experimental import pallas as pl
from jax.experimental.pallas import tpu as pltpu
from jax.sharding import PartitionSpec as P

PASSES = 4
HALO = PASSES + 1
EDGE = 8
NEAR_ONE = 2.0**-6
ROUND = 1.5 * 2.0**23
BOTH = ("lon", "lat")
HIGHEST = lax.Precision.HIGHEST
VMEM = pl.BlockSpec(memory_space=pltpu.VMEM)
ANYWHERE = pl.BlockSpec(memory_space=pl.ANY)
PARAMS = pltpu.CompilerParams(vmem_limit_bytes=24 * 2**20)
SMALL = pltpu.CompilerParams(vmem_limit_bytes=12 * 2**20)


def place():
    lat = lax.axis_index("lat")
    return 1 - lax.rem(lax.axis_index("lon"), 2), lat, lat > 0, lat < lax.axis_size("lat") - 1


def f32(*shape):
    return jax.ShapeDtypeStruct(shape, jnp.float32)


def power_of_two(value):
    scaled = value * (2.0**23 + 1.0)
    return scaled - (scaled - value)


def dot_nt(left, right):
    return lax.dot_general(
        left, right, (((1,), (1,)), ((), ())), preferred_element_type=jnp.float32
    )


def dot_nn(left, right, precision=None):
    return lax.dot_general(
        left,
        right,
        (((1,), (0,)), ((), ())),
        precision=precision,
        preferred_element_type=jnp.float32,
    )


def slices_of(scaled):
    first = (scaled + ROUND) - ROUND
    rest = (scaled - first) * 256.0
    second = (rest + ROUND) - ROUND
    rest = (rest - second) * 256.0
    third = (rest + ROUND) - ROUND
    return first, second, third


def longitude(backwards, row, clon):
    return row + backwards * (clon - 1 - 2 * row)


def prepare_kernel(
    pressure_ref, mask_ref, turned_ref, mask_out_ref, near_ref, far_ref, *end_refs, clon, clat, snaps
):
    edge_refs, near_edge_refs, far_edge_refs = [end_refs[i::3] for i in range(3)]
    backwards, lat, _, _ = place()
    line = lax.broadcasted_iota(jnp.int32, (EDGE, clat), 0)
    for row in range(clon):
        spot = longitude(backwards, row, clon)
        plane = pressure_ref[pl.ds(spot, snaps, stride=clon), :].T
        mask = mask_ref[pl.ds(spot, 1), :]
        turned_ref[row] = plane
        mask_out_ref[row : row + 1] = mask
        low = jnp.where(line < HALO, plane[:EDGE], mask)
        high = jnp.where(line >= EDGE - HALO, plane[clat - EDGE :], mask)
        ends = (low, high) if len(edge_refs) == 2 else (jnp.where(lat == 0, high, low),)
        for edge_ref, end in zip(edge_refs, ends):
            edge_ref[row] = end
        for i, main_ref, side_refs in (
            (row, near_ref, near_edge_refs),
            (clon - 1 - row, far_ref, far_edge_refs),
        ):
            if i < HALO:
                main_ref[i, :clat] = plane
                main_ref[i, clat:] = jnp.broadcast_to(mask, (EDGE, clat))
                for edge_ref, end in zip(side_refs, ends):
                    edge_ref[i] = end


def prepare(pressure, mask, edges):
    snaps, clon, clat = pressure.shape
    body = functools.partial(prepare_kernel, clon=clon, clat=clat, snaps=snaps)
    return pl.pallas_call(
        body,
        out_shape=[f32(clon, clat, snaps), f32(clon, clat)]
        + [f32(HALO, clat + EDGE, snaps)] * 2
        + [f32(clon, EDGE, snaps), f32(HALO, EDGE, snaps), f32(HALO, EDGE, snaps)] * edges,
        in_specs=[VMEM, VMEM],
        compiler_params=SMALL,
        name="prepare",
    )(pressure.reshape(snaps * clon, clat), mask)


def ends_of(left_ref, right_ref, row, has_left, has_right):
    left, right = left_ref[row], right_ref[row]
    return (
        jnp.where(has_left, left, 0.0),
        jnp.where(has_right, right, 0.0),
        jnp.where(has_left, left[:1], 0.0),
        jnp.where(has_right, right[EDGE - 1 :], 0.0),
    )


class Tables:
    def __init__(self, masks, keep_lon, keep_lat, quarter):
        self.masks = masks
        self.keep_lon = keep_lon
        self.keep_lat = keep_lat
        self.quarter = quarter

    def put_masks(self, row, own, left, right):
        for which, value in enumerate((own, left, right)):
            self.masks[which, row : row + 1] = value

    def fill(self, rows, clat):
        padded = self.masks.shape[1]
        own, left, right = self.masks[0], self.masks[1], self.masks[2]
        lane = lax.broadcasted_iota(jnp.int32, (padded, clat), 1)
        first_lane = lane == 0
        last_lane = lane == clat - 1

        def up(mask):
            return pltpu.roll(mask, 1, 1)

        def down(mask):
            return pltpu.roll(mask, clat - 1, 1)

        def coefficients(mask, south, north):
            across = pltpu.roll(mask, 1, 0) + pltpu.roll(mask, padded - 1, 0)
            return (
                mask * (1.0 - 0.25 * across),
                mask * (1.0 - 0.25 * (south + north)),
                0.25 * mask,
            )

        middle = coefficients(
            own,
            jnp.where(first_lane, up(left), up(own)),
            jnp.where(last_lane, down(right), down(own)),
        )
        lower = coefficients(left, up(left), jnp.where(last_lane, down(own), down(left)))
        upper = coefficients(right, jnp.where(first_lane, up(own), up(right)), down(right))
        for which, table in enumerate((self.keep_lon, self.keep_lat, self.quarter)):
            column = jnp.concatenate(
                [lower[which].T[clat - EDGE :], middle[which].T, upper[which].T[:EDGE]], axis=0
            )
            for row in rows:
                table[row] = jnp.broadcast_to(
                    column[:, row : row + 1], (clat + 2 * EDGE, table.shape[2])
                )


def sweep(tables, source, target, swept, begin, end, tall):
    lower, upper = EDGE, EDGE + tall

    def one(row, carry):
        around = source[row - 1, lower:upper] + source[row + 1, lower:upper]
        near = tables.quarter[row]
        middle = tables.keep_lon[row] * source[row, lower:upper] + near * around
        swept[row, lower:upper] = middle
        around = swept[row, lower - 1 : upper - 1] + swept[row, lower + 1 : upper + 1]
        target[row, lower:upper] = tables.keep_lat[row] * middle + near * around
        return carry

    lax.fori_loop(begin, end, one, 0)


def start_row(tables, field, row, ends, middle):
    kept = tables.quarter[row] * 4.0
    clat = middle.shape[0]
    field[row, EDGE : 2 * EDGE] = ends[0] * kept[:EDGE]
    field[row, 2 * EDGE : 2 * EDGE + clat] = middle * kept[EDGE : EDGE + clat]
    field[row, 2 * EDGE + clat : 3 * EDGE + clat] = ends[1] * kept[EDGE + clat :]


def clear_ends(swept, rows, tall, snaps):
    zeros = jnp.zeros((EDGE, snaps), jnp.float32)
    for row in rows:
        swept[row, :EDGE] = zeros
        swept[row, EDGE + tall :] = zeros


def fields_of(backwards, tables, source, planes, rows, offset, clat, snaps):
    begin = 2 * EDGE
    end = begin + clat
    count = len(rows)
    sign = jnp.where(backwards > 0, -2.0, 2.0)

    def one(i, top):
        here = rows[0] + i + offset
        center = source[here, begin:end]
        quarter = tables.quarter[here, EDGE : EDGE + clat]
        along_lon = (quarter * sign) * (source[here + 1, begin:end] - source[here - 1, begin:end])
        along_lat = (quarter * 2.0) * (
            source[here, begin + 1 : end + 1] - source[here, begin - 1 : end - 1]
        )
        for which, value in enumerate((center, along_lon, along_lat)):
            value = value.T
            planes[which * count + i] = value
            top = jnp.maximum(top, jnp.abs(value))
        return top

    return lax.fori_loop(0, count, one, jnp.zeros((snaps, clat), jnp.float32))


def gram_of(planes, count, top, snaps, clat):
    unit = power_of_two(jnp.maximum(jnp.max(top, axis=1, keepdims=True), 2.0**-60))
    to_whole = jnp.broadcast_to(128.0 / unit, (snaps, clat))
    whole = jnp.zeros((snaps, snaps), jnp.int32)
    first_second = jnp.zeros((snaps, snaps), jnp.float32)
    second_any = jnp.zeros((snaps, 2 * snaps), jnp.float32)
    third_any = jnp.zeros((snaps, 2 * snaps), jnp.float32)
    for begin in range(0, count, 2):
        parts = [slices_of(planes[which] * to_whole) for which in range(begin, min(begin + 2, count))]
        a, b, c = [
            jnp.concatenate([piece.astype(jnp.bfloat16) for piece in same], axis=1) for same in zip(*parts)
        ]
        from_first = dot_nt(a, jnp.concatenate([a, b], axis=0))
        whole = whole + from_first[:, :snaps].astype(jnp.int32)
        first_second = first_second + from_first[:, snaps:]
        second_any = second_any + dot_nt(b, jnp.concatenate([b, c], axis=0))
        third_any = third_any + dot_nt(c, jnp.concatenate([a, c], axis=0))
    fine = (
        first_second
        + (second_any[:, :snaps] * 2.0**-9 + second_any[:, snaps:] * 2.0**-16)
        + (third_any[:, :snaps] * 2.0**-8 + third_any[:, snaps:] * 2.0**-25)
    )
    head = whole.astype(jnp.float32)
    tail = (whole - head.astype(jnp.int32)).astype(jnp.float32) + (fine + fine.T) * 2.0**-8
    total = head + tail
    tail = tail - (total - head)
    unit = jnp.broadcast_to(unit * (1.0 / 128.0), (snaps, snaps))
    return total * unit * unit.T, tail * unit * unit.T


def add_pairs(left, right):
    total = left[0] + right[0]
    moved = total - left[0]
    lost = (left[0] - (total - moved)) + (right[0] - moved)
    return total, lost + (left[1] + right[1])


def put_gram(gram_ref, head, tail):
    half = head.shape[0] // 2
    for core in range(2):
        gram_ref[core, 0] = head[core * half : (core + 1) * half]
        gram_ref[core, 1] = tail[core * half : (core + 1) * half]


def near_kernel(
    turned_ref, mask_ref, left_ref, right_ref, near_ref, near_left_ref, near_right_ref,
    x_ref, rim_ref, gram_ref,
    field_a, field_b, swept, masks, keep_lon, keep_lat, quarter, *, clon, clat, snaps,
):
    tall = clat + 2 * EDGE
    lower, upper = EDGE, EDGE + tall
    tables = Tables(masks, keep_lon, keep_lat, quarter)
    wide = clon + HALO
    backwards, _, has_left, has_right = place()
    for i in range(HALO):
        ends = ends_of(near_left_ref, near_right_ref, i, has_left, has_right)
        tables.put_masks(HALO - 1 - i, near_ref[i, clat : clat + 1], *ends[2:])
    for row in range(clon):
        ends = ends_of(left_ref, right_ref, row, has_left, has_right)
        tables.put_masks(HALO + row, mask_ref[row : row + 1], *ends[2:])
    for row in range(wide, masks.shape[1]):
        zero = jnp.zeros((1, clat), jnp.float32)
        tables.put_masks(row, zero, zero, zero)
    tables.fill(range(wide), clat)
    clear_ends(swept, range(wide), tall, snaps)
    for i in range(HALO):
        ends = ends_of(near_left_ref, near_right_ref, i, has_left, has_right)
        start_row(tables, field_a, HALO - 1 - i, ends, near_ref[i, :clat])

    def own_row(row, carry):
        ends = ends_of(left_ref, right_ref, row, has_left, has_right)
        start_row(tables, field_a, row + HALO, ends, turned_ref[row])
        return carry

    lax.fori_loop(0, clon, own_row, 0)
    source, target = field_a, field_b
    for step in range(PASSES + 1):
        rim_ref[step] = source[wide - 2 - step : wide - step, lower:upper]
        if step < PASSES:
            sweep(tables, source, target, swept, step + 1, wide - 1 - step, tall)
            source, target = target, source
    rows = range(clon - HALO)
    top = fields_of(backwards, tables, source, x_ref, rows, HALO, clat, snaps)
    put_gram(gram_ref, *gram_of(x_ref, 3 * len(rows), top, snaps, clat))


def far_kernel(
    mask_ref, left_ref, right_ref, far_ref, far_left_ref, far_right_ref, rim_ref, gram_in_ref,
    x_ref, gram_ref,
    field_a, field_b, swept, masks, keep_lon, keep_lat, quarter, *, clon, clat, snaps,
):
    tall = clat + 2 * EDGE
    lower, upper = EDGE, EDGE + tall
    tables = Tables(masks, keep_lon, keep_lat, quarter)
    backwards, _, has_left, has_right = place()
    skip = clon - HALO - 1
    wide = 2 * HALO + 1
    for row in range(skip, clon):
        ends = ends_of(left_ref, right_ref, row, has_left, has_right)
        tables.put_masks(row - skip, mask_ref[row : row + 1], *ends[2:])
    for i in range(HALO):
        ends = ends_of(far_left_ref, far_right_ref, i, has_left, has_right)
        tables.put_masks(HALO + 1 + i, far_ref[i, clat : clat + 1], *ends[2:])
    for row in range(wide, masks.shape[1]):
        zero = jnp.zeros((1, clat), jnp.float32)
        tables.put_masks(row, zero, zero, zero)
    tables.fill(range(1, wide), clat)
    clear_ends(swept, range(1, wide - 1), tall, snaps)
    for i in range(HALO):
        ends = ends_of(far_left_ref, far_right_ref, i, has_left, has_right)
        start_row(tables, field_a, HALO + 1 + i, ends, far_ref[i, :clat])
    source, target = field_a, field_b
    for step in range(PASSES + 1):
        source[HALO - 1 - step : HALO + 1 - step, lower:upper] = rim_ref[step]
        if step < PASSES:
            sweep(tables, source, target, swept, HALO - step, 2 * HALO - step, tall)
            source, target = target, source
    rows = range(clon - HALO, clon)
    top = fields_of(backwards, tables, source, x_ref, rows, -skip, clat, snaps)
    gram = gram_of(x_ref, 3 * len(rows), top, snaps, clat)
    before = [jnp.concatenate([gram_in_ref[0, part], gram_in_ref[1, part]], axis=0) for part in range(2)]
    put_gram(gram_ref, *add_pairs(before, gram))


def filter_scratch(wide, clat, snaps):
    tall = clat + 2 * EDGE
    field = pltpu.VMEM((wide, tall + 2 * EDGE, snaps), jnp.float32)
    table = pltpu.VMEM((wide, tall, snaps), jnp.float32)
    masks = pltpu.VMEM((3, -(-wide // 8) * 8, clat), jnp.float32)
    return [field, field, field, masks, table, table, table]


def near_part(turned, mask, *halos):
    clon, clat, snaps = turned.shape
    return pl.pallas_call(
        functools.partial(near_kernel, clon=clon, clat=clat, snaps=snaps),
        out_shape=[
            f32(3 * (clon - HALO), snaps, clat),
            f32(PASSES + 1, 2, clat + 2 * EDGE, snaps),
            f32(2, 2, snaps // 2, snaps),
        ],
        in_specs=[VMEM] * 7,
        out_specs=[VMEM, VMEM, VMEM],
        scratch_shapes=filter_scratch(clon + HALO, clat, snaps),
        compiler_params=PARAMS,
        cost_estimate=pl.CostEstimate(flops=4_000_000_000, bytes_accessed=8_000_000, transcendentals=0),
        name="near_part",
    )(turned, mask, *halos)


def far_part(mask, halos, rim, gram, clon, clat, snaps):
    return pl.pallas_call(
        functools.partial(far_kernel, clon=clon, clat=clat, snaps=snaps),
        out_shape=[f32(3 * HALO, snaps, clat), f32(2, 2, snaps // 2, snaps)],
        in_specs=[VMEM] * 8,
        out_specs=[VMEM, VMEM],
        scratch_shapes=filter_scratch(2 * HALO + 1, clat, snaps),
        compiler_params=PARAMS,
        name="far_part",
    )(mask, *halos, rim, gram)


def spread(row, lane):
    return jnp.broadcast_to(row[:, lane : lane + 1], row.shape)


def eliminate(matrix):
    size = matrix.shape[0]
    count = size // 8
    tiles = [matrix[8 * i : 8 * i + 8, :] for i in range(count)]
    lane = lax.broadcasted_iota(jnp.int32, (8, size), 1)
    sub = lax.broadcasted_iota(jnp.int32, (8, size), 0)
    uppers, inverses = [], []

    def every(value, r):
        return jnp.broadcast_to(value[r : r + 1, :], (8, size))

    columns = [spread(tiles[0], c) for c in range(8)]
    for block in range(count):
        base = 8 * block
        panel = tiles[block]
        inside = (lane >= base) & (lane < base + 8)
        rows = [every(panel, r) for r in range(8)]
        entry = {(r, c): every(columns[c], r) for r in range(8) for c in range(r + 1)}
        if block + 1 < count:
            columns = [spread(tiles[block + 1], base + 8 + c) for c in range(8)]
        units = [jnp.where(lane == base + r, 1.0, 0.0) for r in range(8)]
        factor = {}
        pivots = []
        for k in range(8):
            pivots.append(1.0 / entry[k, k])
            for r in range(k + 1, 8):
                factor[r, k] = entry[r, k] * pivots[k]
            for r in range(k + 1, 8):
                for c in range(k + 1, r + 1):
                    entry[r, c] = entry[r, c] - factor[r, k] * entry[c, k]
        for k in range(8):
            for r in range(k + 1, 8):
                rows[r] = rows[r] - factor[r, k] * rows[k]
                units[r] = units[r] - factor[r, k] * units[k]
        joined = [jnp.where(inside, units[r], rows[r]) for r in range(8)]
        for i in range(block + 1, count):
            raw = [spread(tiles[i], base + k) for k in range(8)]
            tile = jnp.where(inside, 0.0, tiles[i])
            for k in range(8):
                scaled = raw[k] * pivots[k]
                for q in range(k + 1, 8):
                    raw[q] = raw[q] - scaled * entry[q, k]
                tile = tile - scaled * joined[k]
                if i == block + 1:
                    columns = [columns[c] - scaled * every(raw[k], c) for c in range(8)]
            tiles[i] = tile
        upper = jnp.zeros((8, size), jnp.float32)
        inverse = jnp.zeros((8, size), jnp.float32)
        for r in range(8):
            scale = lax.rsqrt(entry[r, r])
            upper = jnp.where(sub == r, rows[r] * scale, upper)
            inverse = jnp.where(sub == r, joined[r] * scale, inverse)
        uppers.append(jnp.where(lane >= base + sub, upper, 0.0))
        inverses.append(jnp.where(lane <= base + sub, inverse, 0.0))
    return jnp.concatenate(uppers, axis=0), jnp.concatenate(inverses, axis=0)


def thirds(value):
    first = value.astype(jnp.bfloat16)
    rest = value - first.astype(jnp.float32)
    second = rest.astype(jnp.bfloat16)
    third = (rest - second.astype(jnp.float32)).astype(jnp.bfloat16)
    return first, second, third


def modes_kernel(
    gram_ref, near_ref, far_ref, modes_ref, factor_ref, out_vmem, upper_vmem, combined_vmem, out_sems, *, clon, clat, snaps, total_rows
):
    head, tail = [jnp.concatenate([gram_ref[0, part], gram_ref[1, part]], axis=0) for part in range(2)]
    row = lax.broadcasted_iota(jnp.int32, (snaps, snaps), 0)
    col = lax.broadcasted_iota(jnp.int32, (snaps, snaps), 1)
    diagonal = jnp.where(row == col, head, 0.0)
    grow = power_of_two(jnp.sqrt(jnp.sum(diagonal, axis=1, keepdims=True)))
    shrink_rows = jnp.broadcast_to(1.0 / grow, (snaps, snaps))
    shrink_cols = shrink_rows.T
    head = head * shrink_rows * shrink_cols
    tail = tail * shrink_rows * shrink_cols

    upper_one, inverse_one = eliminate(head)

    first, second, third = slices_of(upper_one.T * 128.0)
    a = first.astype(jnp.bfloat16)
    b = second.astype(jnp.bfloat16)
    c = third.astype(jnp.bfloat16)
    exact = dot_nt(a, a)
    mixed = dot_nt(a, b)
    mixed_small = (
        dot_nt(a, c) + dot_nt(b, b) * 0.5 + dot_nt(b, c) * 2.0**-8 + dot_nt(c, c) * 2.0**-17
    )
    mixed = mixed + mixed.T
    mixed_small = mixed_small + mixed_small.T
    missing = (head - exact * 2.0**-14) - mixed * 2.0**-22
    missing = missing - mixed_small * 2.0**-30 + tail
    lower_one = (first + second * 2.0**-8 + third * 2.0**-16) * (1.0 / 128.0)

    near_one = dot_nn(inverse_one, lower_one, HIGHEST)
    left_over = dot_nn(dot_nn(inverse_one, missing, HIGHEST), inverse_one.T, HIGHEST)
    gram_two = dot_nn(near_one, near_one.T, HIGHEST) + left_over
    gram_two = 0.5 * (gram_two + gram_two.T)
    difference = gram_two - jnp.where(row == col, 1.0, 0.0)

    def lower_half(matrix):
        return jnp.where(row > col, matrix, jnp.where(row == col, 0.5 * matrix, 0.0))

    small = jnp.sum(difference * difference) < NEAR_ONE**2

    @pl.when(small)
    def _():
        k = lower_half(difference)
        for _ in range(2):
            rough = k.astype(jnp.bfloat16)
            k = lower_half(difference - dot_nt(rough, rough))
        rough = k.astype(jnp.bfloat16)
        square = dot_nn(rough, rough)
        change = k - dot_nn(rough, (k - square).astype(jnp.bfloat16))
        upper_vmem[...] = k.T + jnp.where(row == col, 1.0, 0.0)
        combined_vmem[...] = inverse_one - dot_nn(change, inverse_one, HIGHEST)

    @pl.when(jnp.logical_not(small))
    def _():
        upper, inverse = eliminate(gram_two)
        upper_vmem[...] = upper
        combined_vmem[...] = dot_nn(inverse, inverse_one, HIGHEST)

    scale = float(total_rows) ** 0.5
    combined = combined_vmem[...] * shrink_cols * scale
    first, second, third = thirds(combined)
    first_second = jnp.concatenate([first, second], axis=1)
    first_third = jnp.concatenate([first, third], axis=1)
    backwards, _, _, _ = place()
    near_rows = clon - HALO

    def plane(which, q):
        if q < near_rows:
            return near_ref[which * near_rows + q]
        return far_ref[which * HALO + q - near_rows]

    copies = []
    for which in range(3):
        for part in range(clon // 8):
            spot = which * (clon // 8) + part
            flat = out_vmem.at[spot].reshape(snaps * 8, clat)
            for lon in range(0, 8, 2):
                q = part * 8 + lon
                both = jnp.concatenate([plane(which, q), plane(which, q + 1)], axis=1)
                x_one, x_two, x_three = thirds(both)
                value = (
                    dot_nn(first_third, jnp.concatenate([x_three, x_one], axis=0))
                    + dot_nn(first_second, jnp.concatenate([x_two, x_two], axis=0))
                ) + dot_nn(first_second, jnp.concatenate([x_one, x_one], axis=0))
                for side in range(2):
                    to = longitude(backwards, lon + side, 8)
                    flat[pl.ds(to, snaps, stride=8), :] = value[:, side * clat : (side + 1) * clat]
            to = pl.multiple_of(8 * longitude(backwards, part, clon // 8), 8)
            copy = pltpu.make_async_copy(
                out_vmem.at[spot], modes_ref.at[:, which, pl.ds(to, 8), :], out_sems.at[spot]
            )
            copy.start()
            copies.append(copy)
    factor = dot_nn(upper_vmem[...], lower_one.T, HIGHEST) * jnp.broadcast_to(grow, (snaps, snaps)).T
    factor_ref[...] = jnp.where(col >= row, factor * (1.0 / scale), 0.0)
    for copy in copies:
        copy.wait()


def orthonormal(gram, x_near, x_far, clon, clat, total_rows):
    snaps = gram.shape[3]
    parts = 3 * clon // 8
    return pl.pallas_call(
        functools.partial(modes_kernel, clon=clon, clat=clat, snaps=snaps, total_rows=total_rows),
        out_shape=[f32(snaps, 3, clon, clat), f32(snaps, snaps)],
        in_specs=[VMEM] * 3,
        out_specs=[ANYWHERE, VMEM],
        scratch_shapes=[
            pltpu.VMEM((parts, snaps, 8, clat), jnp.float32),
            pltpu.VMEM((snaps, snaps), jnp.float32),
            pltpu.VMEM((snaps, snaps), jnp.float32),
            pltpu.SemaphoreType.DMA((parts,)),
        ],
        compiler_params=PARAMS,
        name="orthonormal",
    )(gram, x_near, x_far)


def summed(halves, nlon, nlat):
    count = nlon * nlat
    core = lax.axis_index("lon") % 2

    def partner(value, step):
        return lax.ppermute(value, BOTH, [(i, i ^ step) for i in range(count)])

    def add(left, right):
        return jnp.stack(add_pairs(left, right))

    mine = add(
        jnp.where(core == 0, halves[0], halves[1]),
        partner(jnp.where(core == 0, halves[1], halves[0]), nlat),
    )
    steps = [1 << bit for bit in range(count.bit_length() - 1) if 1 << bit != nlat]
    while steps:
        if len(steps) >= 2:
            low, high = steps[0], steps[1]
            others = [partner(mine, step) for step in (low, high, low ^ high)]
            mine = add(add(mine, others[0]), add(others[1], others[2]))
            steps = steps[2:]
        else:
            mine = add(mine, partner(mine, steps[0]))
            steps = steps[1:]
    other = partner(mine, nlat)
    return jnp.where(core == 0, jnp.stack([mine, other]), jnp.stack([other, mine]))


def on_device(pressure, ocean_mask):
    snaps, clon, clat = pressure.shape
    nlon, nlat = lax.axis_size("lon"), lax.axis_size("lat")
    merged = nlat == 2
    turned, mask, near, far, *ends = prepare(pressure, ocean_mask.astype(jnp.float32), 1 if merged else 2)

    def partner(i, side):
        return [i, i ^ 1, (i + 1 if i % 2 else i - 1) % nlon][side]

    def move(block, side, shift):
        pairs = []
        for i in range(nlon):
            for j in range(nlat):
                to = 1 - j if shift == 0 else j + shift
                if 0 <= to < nlat:
                    pairs.append((i * nlat + j, partner(i, side) * nlat + to))
        return lax.ppermute(block, BOTH, pairs)

    if merged:
        both = [move(ends[side], side, 0) for side in range(3)]
        both = [(block, block) for block in both]
    else:
        both = [(move(ends[3 + side], side, 1), move(ends[side], side, -1)) for side in range(3)]
    far = lax.ppermute(far, "lon", [(i, partner(i, 2)) for i in range(nlon)])
    near = lax.ppermute(near, "lon", [(i, partner(i, 1)) for i in range(nlon)])
    x_near, rim, gram = near_part(turned, mask, *both[0], near, *both[1])
    x_far, gram = far_part(mask, (*both[0], far, *both[2]), rim, gram, clon, clat, snaps)
    gram = summed(gram, nlon, nlat)
    return tuple(orthonormal(gram, x_near, x_far, clon, clat, 3 * clon * clat * nlon * nlat))


def solution(mesh):
    return jax.shard_map(
        on_device,
        mesh=mesh,
        in_specs=(P(None, "lon", "lat"), P("lon", "lat")),
        out_specs=(P(None, None, "lon", "lat"), P()),
        check_vma=False,
    )
```

```python
import functools

import jax
import jax.numpy as jnp
from jax import lax
from jax.experimental import pallas as pl
from jax.experimental.pallas import tpu as pltpu
from jax.sharding import PartitionSpec as P

PASSES = 4
HALO = PASSES + 1
EDGE = 8
DEPTH = 4
NEAR_ONE = 2.0**-6
ROUND = 1.5 * 2.0**23
BOTH = ("lon", "lat")
HIGHEST = lax.Precision.HIGHEST
VMEM = pl.BlockSpec(memory_space=pltpu.VMEM)
ANYWHERE = pl.BlockSpec(memory_space=pl.ANY)
PARAMS = pltpu.CompilerParams(vmem_limit_bytes=24 * 2**20)
SMALL = pltpu.CompilerParams(vmem_limit_bytes=12 * 2**20)


def place():
    lat = lax.axis_index("lat")
    return 1 - lax.rem(lax.axis_index("lon"), 2), lat, lat > 0, lat < lax.axis_size("lat") - 1


def f32(*shape):
    return jax.ShapeDtypeStruct(shape, jnp.float32)


def power_of_two(value):
    scaled = value * (2.0**23 + 1.0)
    return scaled - (scaled - value)


def dot_nt(left, right):
    return lax.dot_general(
        left, right, (((1,), (1,)), ((), ())), preferred_element_type=jnp.float32
    )


def dot_nn(left, right, precision=None):
    return lax.dot_general(
        left,
        right,
        (((1,), (0,)), ((), ())),
        precision=precision,
        preferred_element_type=jnp.float32,
    )


def slices_of(scaled):
    first = (scaled + ROUND) - ROUND
    rest = scaled - first
    second = (rest + ROUND * 2.0**-8) - ROUND * 2.0**-8
    return first, second, rest - second


def longitude(backwards, row, clon):
    return row + backwards * (clon - 1 - 2 * row)


def plane_of(pressure_ref, mask_ref, row, clon, snaps):
    spot = longitude(place()[0], row, clon)
    return pressure_ref[pl.ds(spot, snaps, stride=clon), :].T, mask_ref[pl.ds(spot, 1), :]


def far_rows_kernel(pressure_ref, mask_ref, far_ref, *, clon, clat, snaps):
    masks = []
    for i in range(HALO):
        plane, mask = plane_of(pressure_ref, mask_ref, clon - 1 - i, clon, snaps)
        far_ref[i * clat : (i + 1) * clat] = plane
        masks.append(mask)
    far_ref[HALO * clat :] = jnp.concatenate(masks + [jnp.zeros((EDGE - HALO, clat), jnp.float32)], axis=0)


def prepare_kernel(
    pressure_ref, mask_ref, far_ref, turned_ref, mask_out_ref, near_ref, *end_refs, clon, clat, snaps
):
    edge_refs, near_edge_refs, far_edge_refs = [end_refs[i::3] for i in range(3)]
    lat = place()[1]
    line = lax.broadcasted_iota(jnp.int32, (EDGE, clat), 0)
    for row in range(clon):
        if row < clon - HALO:
            plane, mask = plane_of(pressure_ref, mask_ref, row, clon, snaps)
        else:
            i = clon - 1 - row
            plane = far_ref[i * clat : (i + 1) * clat]
            mask = far_ref[HALO * clat + i : HALO * clat + i + 1]
        turned_ref[row] = plane
        mask_out_ref[row : row + 1] = mask
        low = jnp.where(line < HALO, plane[:EDGE], mask)
        high = jnp.where(line >= EDGE - HALO, plane[clat - EDGE :], mask)
        ends = (low, high) if len(edge_refs) == 2 else (jnp.where(lat == 0, high, low),)
        for edge_ref, end in zip(edge_refs, ends):
            edge_ref[row] = end
        for i, side_refs in ((row, near_edge_refs), (clon - 1 - row, far_edge_refs)):
            if i < HALO:
                for edge_ref, end in zip(side_refs, ends):
                    edge_ref[i] = end
        if row < HALO:
            near_ref[row * clat : (row + 1) * clat] = plane
            near_ref[HALO * clat + row : HALO * clat + row + 1] = mask


def prepare(pressure, mask, edges):
    snaps, clon, clat = pressure.shape
    sizes = dict(clon=clon, clat=clat, snaps=snaps)
    rows = f32(HALO * clat + EDGE, snaps)
    inputs = (pressure.reshape(snaps * clon, clat), mask)
    far = pl.pallas_call(
        functools.partial(far_rows_kernel, **sizes),
        out_shape=rows,
        in_specs=[VMEM, VMEM],
        compiler_params=SMALL,
        name="far_rows",
    )(*inputs)
    turned, mask, near, *ends = pl.pallas_call(
        functools.partial(prepare_kernel, **sizes),
        out_shape=[f32(clon, clat, snaps), f32(clon, clat), rows]
        + [f32(clon, EDGE, snaps), f32(HALO, EDGE, snaps), f32(HALO, EDGE, snaps)] * edges,
        in_specs=[VMEM, VMEM, VMEM],
        compiler_params=SMALL,
        name="prepare",
    )(*inputs, far)
    return turned, mask, near, far, ends


def ends_of(left_ref, right_ref, row, has_left, has_right):
    left, right = left_ref[row], right_ref[row]
    return (
        jnp.where(has_left, left, 0.0),
        jnp.where(has_right, right, 0.0),
        jnp.where(has_left, left[:1], 0.0),
        jnp.where(has_right, right[EDGE - 1 :], 0.0),
    )


class Tables:
    def __init__(self, masks, keep_lon, keep_lat, quarter):
        self.masks = masks
        self.keep_lon = keep_lon
        self.keep_lat = keep_lat
        self.quarter = quarter

    def put_masks(self, row, own, left, right):
        for which, value in enumerate((own, left, right)):
            self.masks[which, row : row + 1] = value

    def fill(self, rows, clat):
        padded = self.masks.shape[1]
        own, left, right = self.masks[0], self.masks[1], self.masks[2]
        lane = lax.broadcasted_iota(jnp.int32, (padded, clat), 1)
        first_lane = lane == 0
        last_lane = lane == clat - 1

        def up(mask):
            return pltpu.roll(mask, 1, 1)

        def down(mask):
            return pltpu.roll(mask, clat - 1, 1)

        def coefficients(mask, south, north):
            across = pltpu.roll(mask, 1, 0) + pltpu.roll(mask, padded - 1, 0)
            return (
                mask * (1.0 - 0.25 * across),
                mask * (1.0 - 0.25 * (south + north)),
            )

        middle = coefficients(
            own,
            jnp.where(first_lane, up(left), up(own)),
            jnp.where(last_lane, down(right), down(own)),
        )
        lower = coefficients(left, up(left), jnp.where(last_lane, down(own), down(left)))
        upper = coefficients(right, jnp.where(first_lane, up(own), up(right)), down(right))
        for which, table in enumerate((self.keep_lon, self.keep_lat)):
            column = jnp.concatenate(
                [lower[which].T[clat - EDGE :], middle[which].T, upper[which].T[:EDGE]], axis=0
            )
            for row in rows:
                spread_out = jnp.broadcast_to(column[:, row : row + 1], (clat + 2 * EDGE, table.shape[2]))
                table[row] = spread_out
                if which == 0:
                    self.quarter[row] = jnp.where(spread_out > 0.0, 0.25, 0.0)


def sweep(tables, source, target, swept, begin, end, tall):
    lower, upper = EDGE, EDGE + tall

    def one(row, carry):
        around = source[row - 1, lower:upper] + source[row + 1, lower:upper]
        near = tables.quarter[row]
        middle = tables.keep_lon[row] * source[row, lower:upper] + near * around
        swept[row, lower:upper] = middle
        around = swept[row, lower - 1 : upper - 1] + swept[row, lower + 1 : upper + 1]
        target[row, lower:upper] = tables.keep_lat[row] * middle + near * around
        return carry

    lax.fori_loop(begin, end, one, 0, unroll=True)


def start_row(tables, field, row, ends, middle):
    kept = tables.quarter[row] * 4.0
    clat = middle.shape[0]
    field[row, EDGE : 2 * EDGE] = ends[0] * kept[:EDGE]
    field[row, 2 * EDGE : 2 * EDGE + clat] = middle * kept[EDGE : EDGE + clat]
    field[row, 2 * EDGE + clat : 3 * EDGE + clat] = ends[1] * kept[EDGE + clat :]


def clear_ends(swept, rows, tall, snaps):
    zeros = jnp.zeros((EDGE, snaps), jnp.float32)
    for row in rows:
        swept[row, :EDGE] = zeros
        swept[row, EDGE + tall :] = zeros


def fields_and_gram(backwards, tables, source, planes, rows, offset, clat, snaps):
    begin = 2 * EDGE
    end = begin + clat
    count = len(rows)
    first = rows[0] + offset
    sign = jnp.where(backwards > 0, -2.0, 2.0)

    top = jnp.zeros((clat + 2 * EDGE, snaps), jnp.float32)
    for i in range(count + 2):
        top = jnp.maximum(top, jnp.abs(source[first - 1 + i, EDGE : end + EDGE]))
    unit = power_of_two(jnp.maximum(jnp.max(top, axis=0, keepdims=True), 2.0**-60))
    to_whole = jnp.broadcast_to(128.0 / unit, (clat, snaps)).T

    whole = jnp.zeros((snaps, snaps), jnp.int32)
    first_second = jnp.zeros((snaps, snaps), jnp.float32)
    second_any = jnp.zeros((snaps, 2 * snaps), jnp.float32)
    third_any = jnp.zeros((snaps, 2 * snaps), jnp.float32)
    parts = []
    for i in range(count):
        here = first + i
        quarter = tables.quarter[here, EDGE : EDGE + clat]
        along_lon = (quarter * sign) * (source[here + 1, begin:end] - source[here - 1, begin:end])
        along_lat = (quarter * 2.0) * (
            source[here, begin + 1 : end + 1] - source[here, begin - 1 : end - 1]
        )
        for which, value in enumerate((source[here, begin:end], along_lon, along_lat)):
            value = value.T
            planes[which * count + i] = value
            parts.append([piece.astype(jnp.bfloat16) for piece in slices_of(value * to_whole)])
            if len(parts) < DEPTH and not (i == count - 1 and which == 2):
                continue
            a, b, c = [jnp.concatenate(same, axis=1) for same in zip(*parts)]
            parts = []
            from_first = dot_nt(a, jnp.concatenate([a, b], axis=0))
            whole = whole + from_first[:, :snaps].astype(jnp.int32)
            first_second = first_second + from_first[:, snaps:]
            second_any = second_any + dot_nt(b, jnp.concatenate([b, c], axis=0))
            third_any = third_any + dot_nt(c, jnp.concatenate([a, c], axis=0))
    fine = (
        first_second
        + (second_any[:, :snaps] * 0.5 + second_any[:, snaps:])
        + (third_any[:, :snaps] + third_any[:, snaps:] * 0.5)
    )
    head = whole.astype(jnp.float32)
    tail = (whole - head.astype(jnp.int32)).astype(jnp.float32) + (fine + fine.T)
    total = head + tail
    tail = tail - (total - head)
    unit = jnp.broadcast_to(unit * (1.0 / 128.0), (snaps, snaps))
    scale = unit * unit.T
    return total * scale, tail * scale


def add_pairs(left, right):
    total = left[0] + right[0]
    moved = total - left[0]
    lost = (left[0] - (total - moved)) + (right[0] - moved)
    return total, lost + (left[1] + right[1])


def put_gram(gram_ref, head, tail):
    half = head.shape[0] // 2
    for core in range(2):
        gram_ref[core, 0] = head[core * half : (core + 1) * half]
        gram_ref[core, 1] = tail[core * half : (core + 1) * half]


def near_kernel(
    turned_ref, mask_ref, left_ref, right_ref, near_ref, near_left_ref, near_right_ref,
    x_ref, rim_ref, gram_ref,
    field_a, field_b, swept, masks, keep_lon, keep_lat, quarter, *, clon, clat, snaps,
):
    tall = clat + 2 * EDGE
    lower, upper = EDGE, EDGE + tall
    tables = Tables(masks, keep_lon, keep_lat, quarter)
    wide = clon + HALO
    backwards, _, has_left, has_right = place()
    for i in range(HALO):
        ends = ends_of(near_left_ref, near_right_ref, i, has_left, has_right)
        tables.put_masks(HALO - 1 - i, near_ref[HALO * clat + i : HALO * clat + i + 1], *ends[2:])
    for row in range(clon):
        ends = ends_of(left_ref, right_ref, row, has_left, has_right)
        tables.put_masks(HALO + row, mask_ref[row : row + 1], *ends[2:])
    for row in range(wide, masks.shape[1]):
        zero = jnp.zeros((1, clat), jnp.float32)
        tables.put_masks(row, zero, zero, zero)
    tables.fill(range(wide), clat)
    clear_ends(swept, range(wide), tall, snaps)
    for i in range(HALO):
        ends = ends_of(near_left_ref, near_right_ref, i, has_left, has_right)
        start_row(tables, field_a, HALO - 1 - i, ends, near_ref[i * clat : (i + 1) * clat])

    def own_row(row, carry):
        ends = ends_of(left_ref, right_ref, row, has_left, has_right)
        start_row(tables, field_a, row + HALO, ends, turned_ref[row])
        return carry

    lax.fori_loop(0, clon, own_row, 0)
    source, target = field_a, field_b
    for step in range(PASSES + 1):
        rim_ref[step] = source[wide - 2 - step : wide - step, lower:upper]
        if step < PASSES:
            sweep(tables, source, target, swept, step + 1, wide - 1 - step, tall)
            source, target = target, source
    rows = range(clon - HALO)
    put_gram(gram_ref, *fields_and_gram(backwards, tables, source, x_ref, rows, HALO, clat, snaps))


def far_kernel(
    mask_ref, left_ref, right_ref, far_ref, far_left_ref, far_right_ref, rim_ref, gram_in_ref,
    x_ref, gram_ref,
    field_a, field_b, swept, masks, keep_lon, keep_lat, quarter, *, clon, clat, snaps,
):
    tall = clat + 2 * EDGE
    lower, upper = EDGE, EDGE + tall
    tables = Tables(masks, keep_lon, keep_lat, quarter)
    backwards, _, has_left, has_right = place()
    skip = clon - HALO - 1
    wide = 2 * HALO + 1
    for row in range(skip, clon):
        ends = ends_of(left_ref, right_ref, row, has_left, has_right)
        tables.put_masks(row - skip, mask_ref[row : row + 1], *ends[2:])
    for i in range(HALO):
        ends = ends_of(far_left_ref, far_right_ref, i, has_left, has_right)
        tables.put_masks(HALO + 1 + i, far_ref[HALO * clat + i : HALO * clat + i + 1], *ends[2:])
    for row in range(wide, masks.shape[1]):
        zero = jnp.zeros((1, clat), jnp.float32)
        tables.put_masks(row, zero, zero, zero)
    tables.fill(range(1, wide), clat)
    clear_ends(swept, range(1, wide - 1), tall, snaps)
    for i in range(HALO):
        ends = ends_of(far_left_ref, far_right_ref, i, has_left, has_right)
        start_row(tables, field_a, HALO + 1 + i, ends, far_ref[i * clat : (i + 1) * clat])
    source, target = field_a, field_b
    for step in range(PASSES + 1):
        source[HALO - 1 - step : HALO + 1 - step, lower:upper] = rim_ref[step]
        if step < PASSES:
            sweep(tables, source, target, swept, HALO - step, 2 * HALO - step, tall)
            source, target = target, source
    rows = range(clon - HALO, clon)
    gram = fields_and_gram(backwards, tables, source, x_ref, rows, -skip, clat, snaps)
    before = [jnp.concatenate([gram_in_ref[0, part], gram_in_ref[1, part]], axis=0) for part in range(2)]
    put_gram(gram_ref, *add_pairs(before, gram))


def filter_scratch(wide, clat, snaps):
    tall = clat + 2 * EDGE
    field = pltpu.VMEM((wide, tall + 2 * EDGE, snaps), jnp.float32)
    table = pltpu.VMEM((wide, tall, snaps), jnp.float32)
    masks = pltpu.VMEM((3, -(-wide // 8) * 8, clat), jnp.float32)
    return [field, field, field, masks, table, table, table]


def near_part(turned, mask, *halos):
    clon, clat, snaps = turned.shape
    return pl.pallas_call(
        functools.partial(near_kernel, clon=clon, clat=clat, snaps=snaps),
        out_shape=[
            f32(3 * (clon - HALO), snaps, clat),
            f32(PASSES + 1, 2, clat + 2 * EDGE, snaps),
            f32(2, 2, snaps // 2, snaps),
        ],
        in_specs=[VMEM] * 7,
        out_specs=[VMEM, VMEM, VMEM],
        scratch_shapes=filter_scratch(clon + HALO, clat, snaps),
        compiler_params=PARAMS,
        cost_estimate=pl.CostEstimate(flops=4_000_000_000, bytes_accessed=8_000_000, transcendentals=0),
        name="near_part",
    )(turned, mask, *halos)


def far_part(mask, halos, rim, gram, clon, clat, snaps):
    return pl.pallas_call(
        functools.partial(far_kernel, clon=clon, clat=clat, snaps=snaps),
        out_shape=[f32(3 * HALO, snaps, clat), f32(2, 2, snaps // 2, snaps)],
        in_specs=[VMEM] * 8,
        out_specs=[VMEM, VMEM],
        scratch_shapes=filter_scratch(2 * HALO + 1, clat, snaps),
        compiler_params=PARAMS,
        name="far_part",
    )(mask, *halos, rim, gram)


def spread(row, lane):
    return jnp.broadcast_to(row[:, lane : lane + 1], row.shape)


def eliminate(matrix):
    size = matrix.shape[0]
    count = size // 8
    tiles = [matrix[8 * i : 8 * i + 8, :] for i in range(count)]
    lane = lax.broadcasted_iota(jnp.int32, (8, size), 1)
    sub = lax.broadcasted_iota(jnp.int32, (8, size), 0)
    uppers, inverses = [], []

    def every(value, r):
        return jnp.broadcast_to(value[r : r + 1, :], (8, size))

    columns = [spread(tiles[0], c) for c in range(8)]
    for block in range(count):
        base = 8 * block
        panel = tiles[block]
        inside = (lane >= base) & (lane < base + 8)
        rows = [every(panel, r) for r in range(8)]
        entry = {(r, c): every(columns[c], r) for r in range(8) for c in range(r + 1)}
        if block + 1 < count:
            columns = [spread(tiles[block + 1], base + 8 + c) for c in range(8)]
        units = [jnp.where(lane == base + r, 1.0, 0.0) for r in range(8)]
        factor = {}
        pivots = []
        for k in range(8):
            pivots.append(1.0 / entry[k, k])
            for r in range(k + 1, 8):
                factor[r, k] = entry[r, k] * pivots[k]
            for r in range(k + 1, 8):
                for c in range(k + 1, r + 1):
                    entry[r, c] = entry[r, c] - factor[r, k] * entry[c, k]
        for k in range(8):
            for r in range(k + 1, 8):
                rows[r] = rows[r] - factor[r, k] * rows[k]
                units[r] = units[r] - factor[r, k] * units[k]
        joined = [jnp.where(inside, units[r], rows[r]) for r in range(8)]
        for i in range(block + 1, count):
            raw = [spread(tiles[i], base + k) for k in range(8)]
            tile = jnp.where(inside, 0.0, tiles[i])
            for k in range(8):
                scaled = raw[k] * pivots[k]
                for q in range(k + 1, 8):
                    raw[q] = raw[q] - scaled * entry[q, k]
                tile = tile - scaled * joined[k]
                if i == block + 1:
                    columns = [columns[c] - scaled * every(raw[k], c) for c in range(8)]
            tiles[i] = tile
        upper = jnp.zeros((8, size), jnp.float32)
        inverse = jnp.zeros((8, size), jnp.float32)
        for r in range(8):
            scale = lax.rsqrt(entry[r, r])
            upper = jnp.where(sub == r, rows[r] * scale, upper)
            inverse = jnp.where(sub == r, joined[r] * scale, inverse)
        uppers.append(jnp.where(lane >= base + sub, upper, 0.0))
        inverses.append(jnp.where(lane <= base + sub, inverse, 0.0))
    return jnp.concatenate(uppers, axis=0), jnp.concatenate(inverses, axis=0)


def thirds(value):
    first = value.astype(jnp.bfloat16)
    rest = value - first.astype(jnp.float32)
    second = rest.astype(jnp.bfloat16)
    third = (rest - second.astype(jnp.float32)).astype(jnp.bfloat16)
    return first, second, third


def modes_kernel(
    gram_ref, near_ref, far_ref, modes_ref, factor_ref, out_vmem, upper_vmem, combined_vmem, out_sems, *, clon, clat, snaps, total_rows
):
    head, tail = [jnp.concatenate([gram_ref[0, part], gram_ref[1, part]], axis=0) for part in range(2)]
    row = lax.broadcasted_iota(jnp.int32, (snaps, snaps), 0)
    col = lax.broadcasted_iota(jnp.int32, (snaps, snaps), 1)
    diagonal = jnp.where(row == col, head, 0.0)
    grow = power_of_two(jnp.sqrt(jnp.sum(diagonal, axis=1, keepdims=True)))
    shrink_rows = jnp.broadcast_to(1.0 / grow, (snaps, snaps))
    shrink_cols = shrink_rows.T
    head = head * shrink_rows * shrink_cols
    tail = tail * shrink_rows * shrink_cols

    upper_one, inverse_one = eliminate(head)

    first, second, third = slices_of(upper_one.T * 128.0)
    a = first.astype(jnp.bfloat16)
    b = second.astype(jnp.bfloat16)
    c = third.astype(jnp.bfloat16)
    exact = dot_nt(a, a)
    mixed = dot_nt(a, b)
    mixed_small = dot_nt(a, c) + dot_nt(b, b) * 0.5 + dot_nt(b, c) + dot_nt(c, c) * 0.5
    mixed = mixed + mixed.T
    mixed_small = mixed_small + mixed_small.T
    missing = (head - exact * 2.0**-14) - mixed * 2.0**-14
    missing = missing - mixed_small * 2.0**-14 + tail
    lower_one = (first + second + c.astype(jnp.float32)) * (1.0 / 128.0)

    near_one = dot_nn(inverse_one, lower_one, HIGHEST)
    left_over = dot_nn(dot_nn(inverse_one, missing, HIGHEST), inverse_one.T, HIGHEST)
    gram_two = dot_nn(near_one, near_one.T, HIGHEST) + left_over
    gram_two = 0.5 * (gram_two + gram_two.T)
    difference = gram_two - jnp.where(row == col, 1.0, 0.0)

    def lower_half(matrix):
        return jnp.where(row > col, matrix, jnp.where(row == col, 0.5 * matrix, 0.0))

    small = jnp.sum(difference * difference) < NEAR_ONE**2

    @pl.when(small)
    def _():
        k = lower_half(difference)
        for _ in range(2):
            rough = k.astype(jnp.bfloat16)
            k = lower_half(difference - dot_nt(rough, rough))
        rough = k.astype(jnp.bfloat16)
        square = dot_nn(rough, rough)
        change = k - dot_nn(rough, (k - square).astype(jnp.bfloat16))
        upper_vmem[...] = k.T + jnp.where(row == col, 1.0, 0.0)
        combined_vmem[...] = inverse_one - dot_nn(change, inverse_one, HIGHEST)

    @pl.when(jnp.logical_not(small))
    def _():
        upper, inverse = eliminate(gram_two)
        upper_vmem[...] = upper
        combined_vmem[...] = dot_nn(inverse, inverse_one, HIGHEST)

    scale = float(total_rows) ** 0.5
    combined = combined_vmem[...] * shrink_cols * scale
    first, second, third = thirds(combined)
    first_second = jnp.concatenate([first, second], axis=1)
    first_third = jnp.concatenate([first, third], axis=1)
    backwards, _, _, _ = place()
    near_rows = clon - HALO

    def plane(which, q):
        if q < near_rows:
            return near_ref[which * near_rows + q]
        return far_ref[which * HALO + q - near_rows]

    copies = []
    for which in range(3):
        for part in range(clon // 8):
            spot = which * (clon // 8) + part
            flat = out_vmem.at[spot].reshape(snaps * 8, clat)
            for lon in range(0, 8, 2):
                q = part * 8 + lon
                both = jnp.concatenate([plane(which, q), plane(which, q + 1)], axis=1)
                x_one, x_two, x_three = thirds(both)
                value = (
                    dot_nn(first_third, jnp.concatenate([x_three, x_one], axis=0))
                    + dot_nn(first_second, jnp.concatenate([x_two, x_two], axis=0))
                ) + dot_nn(first_second, jnp.concatenate([x_one, x_one], axis=0))
                for side in range(2):
                    to = longitude(backwards, lon + side, 8)
                    flat[pl.ds(to, snaps, stride=8), :] = value[:, side * clat : (side + 1) * clat]
            to = pl.multiple_of(8 * longitude(backwards, part, clon // 8), 8)
            copy = pltpu.make_async_copy(
                out_vmem.at[spot], modes_ref.at[:, which, pl.ds(to, 8), :], out_sems.at[spot]
            )
            copy.start()
            copies.append(copy)
    factor = dot_nn(upper_vmem[...], lower_one.T, HIGHEST) * jnp.broadcast_to(grow, (snaps, snaps)).T
    factor_ref[...] = jnp.where(col >= row, factor * (1.0 / scale), 0.0)
    for copy in copies:
        copy.wait()


def orthonormal(gram, x_near, x_far, clon, clat, total_rows):
    snaps = gram.shape[3]
    parts = 3 * clon // 8
    return pl.pallas_call(
        functools.partial(modes_kernel, clon=clon, clat=clat, snaps=snaps, total_rows=total_rows),
        out_shape=[f32(snaps, 3, clon, clat), f32(snaps, snaps)],
        in_specs=[VMEM] * 3,
        out_specs=[ANYWHERE, VMEM],
        scratch_shapes=[
            pltpu.VMEM((parts, snaps, 8, clat), jnp.float32),
            pltpu.VMEM((snaps, snaps), jnp.float32),
            pltpu.VMEM((snaps, snaps), jnp.float32),
            pltpu.SemaphoreType.DMA((parts,)),
        ],
        compiler_params=PARAMS,
        name="orthonormal",
    )(gram, x_near, x_far)


def summed(halves, nlon, nlat):
    count = nlon * nlat
    core = lax.axis_index("lon") % 2

    def partner(value, step):
        return lax.ppermute(value, BOTH, [(i, i ^ step) for i in range(count)])

    def add(left, right):
        return jnp.stack(add_pairs(left, right))

    mine = add(
        jnp.where(core == 0, halves[0], halves[1]),
        partner(jnp.where(core == 0, halves[1], halves[0]), nlat),
    )
    steps = [1 << bit for bit in range(count.bit_length() - 1) if 1 << bit != nlat]
    while steps:
        if len(steps) >= 2:
            low, high = steps[0], steps[1]
            others = [partner(mine, step) for step in (low, high, low ^ high)]
            mine = add(add(mine, others[0]), add(others[1], others[2]))
            steps = steps[2:]
        else:
            mine = add(mine, partner(mine, steps[0]))
            steps = steps[1:]
    other = partner(mine, nlat)
    return jnp.where(core == 0, jnp.stack([mine, other]), jnp.stack([other, mine]))


def on_device(pressure, ocean_mask):
    snaps, clon, clat = pressure.shape
    nlon, nlat = lax.axis_size("lon"), lax.axis_size("lat")
    merged = nlat == 2
    turned, mask, near, far, ends = prepare(pressure, ocean_mask.astype(jnp.float32), 1 if merged else 2)

    def partner(i, side):
        return [i, i ^ 1, (i + 1 if i % 2 else i - 1) % nlon][side]

    def move(block, side, shift):
        pairs = []
        for i in range(nlon):
            for j in range(nlat):
                to = 1 - j if shift == 0 else j + shift
                if 0 <= to < nlat:
                    pairs.append((i * nlat + j, partner(i, side) * nlat + to))
        return lax.ppermute(block, BOTH, pairs)

    if merged:
        both = [move(ends[side], side, 0) for side in range(3)]
        both = [(block, block) for block in both]
    else:
        both = [(move(ends[3 + side], side, 1), move(ends[side], side, -1)) for side in range(3)]
    far = lax.ppermute(far, "lon", [(i, partner(i, 2)) for i in range(nlon)])
    near = lax.ppermute(near, "lon", [(i, partner(i, 1)) for i in range(nlon)])
    x_near, rim, gram = near_part(turned, mask, *both[0], near, *both[1])
    x_far, gram = far_part(mask, (*both[0], far, *both[2]), rim, gram, clon, clat, snaps)
    gram = summed(gram, nlon, nlat)
    return tuple(orthonormal(gram, x_near, x_far, clon, clat, 3 * clon * clat * nlon * nlat))


def solution(mesh):
    return jax.shard_map(
        on_device,
        mesh=mesh,
        in_specs=(P(None, "lon", "lat"), P("lon", "lat")),
        out_specs=(P(None, None, "lon", "lat"), P()),
        check_vma=False,
    )
```

```python
import functools

import jax
import jax.numpy as jnp
from jax import lax
from jax.experimental import pallas as pl
from jax.experimental.pallas import tpu as pltpu
from jax.sharding import PartitionSpec as P

PASSES = 4
HALO = PASSES + 1
EDGE = 8
DEPTH = 4
NEAR_ONE = 2.0**-6
ROUND = 1.5 * 2.0**23
BOTH = ("lon", "lat")
HIGHEST = lax.Precision.HIGHEST
VMEM = pl.BlockSpec(memory_space=pltpu.VMEM)
ANYWHERE = pl.BlockSpec(memory_space=pl.ANY)
PARAMS = pltpu.CompilerParams(vmem_limit_bytes=24 * 2**20)
SMALL = pltpu.CompilerParams(vmem_limit_bytes=12 * 2**20)


def place():
    lat = lax.axis_index("lat")
    return 1 - lax.rem(lax.axis_index("lon"), 2), lat, lat > 0, lat < lax.axis_size("lat") - 1


def f32(*shape):
    return jax.ShapeDtypeStruct(shape, jnp.float32)


def power_of_two(value):
    scaled = value * (2.0**23 + 1.0)
    return scaled - (scaled - value)


def dot_nt(left, right):
    return lax.dot_general(
        left, right, (((1,), (1,)), ((), ())), preferred_element_type=jnp.float32
    )


def dot_nn(left, right, precision=None):
    return lax.dot_general(
        left,
        right,
        (((1,), (0,)), ((), ())),
        precision=precision,
        preferred_element_type=jnp.float32,
    )


def slices_of(scaled):
    first = (scaled + ROUND) - ROUND
    rest = scaled - first
    second = (rest + ROUND * 2.0**-8) - ROUND * 2.0**-8
    return first, second, rest - second


def longitude(backwards, row, clon):
    return row + backwards * (clon - 1 - 2 * row)


def plane_of(pressure_ref, mask_ref, row, clon, snaps):
    spot = longitude(place()[0], row, clon)
    return pressure_ref[pl.ds(spot, snaps, stride=clon), :].T, mask_ref[pl.ds(spot, 1), :]


def far_rows_kernel(pressure_ref, mask_ref, far_ref, *, clon, clat, snaps):
    masks = []
    for i in range(HALO):
        plane, mask = plane_of(pressure_ref, mask_ref, clon - 1 - i, clon, snaps)
        far_ref[i * clat : (i + 1) * clat] = plane
        masks.append(mask)
    far_ref[HALO * clat :] = jnp.concatenate(masks + [jnp.zeros((EDGE - HALO, clat), jnp.float32)], axis=0)


def prepare_kernel(
    pressure_ref, mask_ref, far_ref, turned_ref, mask_out_ref, near_ref, *end_refs, clon, clat, snaps
):
    edge_refs, near_edge_refs, far_edge_refs = [end_refs[i::3] for i in range(3)]
    lat = place()[1]
    line = lax.broadcasted_iota(jnp.int32, (EDGE, clat), 0)
    for row in range(clon):
        if row < clon - HALO:
            plane, mask = plane_of(pressure_ref, mask_ref, row, clon, snaps)
        else:
            i = clon - 1 - row
            plane = far_ref[i * clat : (i + 1) * clat]
            mask = far_ref[HALO * clat + i : HALO * clat + i + 1]
        turned_ref[row] = plane
        mask_out_ref[row : row + 1] = mask
        low = jnp.where(line < HALO, plane[:EDGE], mask)
        high = jnp.where(line >= EDGE - HALO, plane[clat - EDGE :], mask)
        ends = (low, high) if len(edge_refs) == 2 else (jnp.where(lat == 0, high, low),)
        for edge_ref, end in zip(edge_refs, ends):
            edge_ref[row] = end
        for i, side_refs in ((row, near_edge_refs), (clon - 1 - row, far_edge_refs)):
            if i < HALO:
                for edge_ref, end in zip(side_refs, ends):
                    edge_ref[i] = end
        if row < HALO:
            near_ref[row * clat : (row + 1) * clat] = plane
            near_ref[HALO * clat + row : HALO * clat + row + 1] = mask


def prepare(pressure, mask, edges):
    snaps, clon, clat = pressure.shape
    sizes = dict(clon=clon, clat=clat, snaps=snaps)
    rows = f32(HALO * clat + EDGE, snaps)
    inputs = (pressure.reshape(snaps * clon, clat), mask)
    far = pl.pallas_call(
        functools.partial(far_rows_kernel, **sizes),
        out_shape=rows,
        in_specs=[VMEM, VMEM],
        compiler_params=SMALL,
        name="far_rows",
    )(*inputs)
    turned, mask, near, *ends = pl.pallas_call(
        functools.partial(prepare_kernel, **sizes),
        out_shape=[f32(clon, clat, snaps), f32(clon, clat), rows]
        + [f32(clon, EDGE, snaps), f32(HALO, EDGE, snaps), f32(HALO, EDGE, snaps)] * edges,
        in_specs=[VMEM, VMEM, VMEM],
        compiler_params=SMALL,
        name="prepare",
    )(*inputs, far)
    return turned, mask, near, far, ends


def ends_of(left_ref, right_ref, row, has_left, has_right):
    left, right = left_ref[row], right_ref[row]
    return (
        jnp.where(has_left, left, 0.0),
        jnp.where(has_right, right, 0.0),
        jnp.where(has_left, left[:1], 0.0),
        jnp.where(has_right, right[EDGE - 1 :], 0.0),
    )


class Tables:
    def __init__(self, masks, keep_lon, keep_lat, quarter):
        self.masks = masks
        self.keep_lon = keep_lon
        self.keep_lat = keep_lat
        self.quarter = quarter

    def put_masks(self, row, own, left, right):
        for which, value in enumerate((own, left, right)):
            self.masks[which, row : row + 1] = value

    def fill(self, rows, clat):
        padded = self.masks.shape[1]
        own, left, right = self.masks[0], self.masks[1], self.masks[2]
        lane = lax.broadcasted_iota(jnp.int32, (padded, clat), 1)
        first_lane = lane == 0
        last_lane = lane == clat - 1

        def up(mask):
            return pltpu.roll(mask, 1, 1)

        def down(mask):
            return pltpu.roll(mask, clat - 1, 1)

        def coefficients(mask, south, north):
            across = pltpu.roll(mask, 1, 0) + pltpu.roll(mask, padded - 1, 0)
            return (
                mask * (1.0 - 0.25 * across),
                mask * (1.0 - 0.25 * (south + north)),
            )

        middle = coefficients(
            own,
            jnp.where(first_lane, up(left), up(own)),
            jnp.where(last_lane, down(right), down(own)),
        )
        lower = coefficients(left, up(left), jnp.where(last_lane, down(own), down(left)))
        upper = coefficients(right, jnp.where(first_lane, up(own), up(right)), down(right))
        for which, table in enumerate((self.keep_lon, self.keep_lat)):
            column = jnp.concatenate(
                [lower[which].T[clat - EDGE :], middle[which].T, upper[which].T[:EDGE]], axis=0
            )
            for row in rows:
                spread_out = jnp.broadcast_to(column[:, row : row + 1], (clat + 2 * EDGE, table.shape[2]))
                table[row] = spread_out
                if which == 0:
                    self.quarter[row] = jnp.where(spread_out > 0.0, 0.25, 0.0)


def sweep(tables, source, target, swept, begin, end, tall):
    lower, upper = EDGE, EDGE + tall

    def one(row, carry):
        around = source[row - 1, lower:upper] + source[row + 1, lower:upper]
        near = tables.quarter[row]
        middle = tables.keep_lon[row] * source[row, lower:upper] + near * around
        swept[row, lower:upper] = middle
        around = swept[row, lower - 1 : upper - 1] + swept[row, lower + 1 : upper + 1]
        target[row, lower:upper] = tables.keep_lat[row] * middle + near * around
        return carry

    lax.fori_loop(begin, end, one, 0, unroll=True)


def start_row(tables, field, row, ends, middle):
    kept = tables.quarter[row] * 4.0
    clat = middle.shape[0]
    field[row, EDGE : 2 * EDGE] = ends[0] * kept[:EDGE]
    field[row, 2 * EDGE : 2 * EDGE + clat] = middle * kept[EDGE : EDGE + clat]
    field[row, 2 * EDGE + clat : 3 * EDGE + clat] = ends[1] * kept[EDGE + clat :]


def clear_ends(swept, rows, tall, snaps):
    zeros = jnp.zeros((EDGE, snaps), jnp.float32)
    for row in rows:
        swept[row, :EDGE] = zeros
        swept[row, EDGE + tall :] = zeros


def fields_and_gram(backwards, tables, source, planes, rows, offset, clat, snaps):
    begin = 2 * EDGE
    end = begin + clat
    count = len(rows)
    first = rows[0] + offset
    sign = jnp.where(backwards > 0, -2.0, 2.0)

    top = jnp.zeros((clat + 2 * EDGE, snaps), jnp.float32)
    for i in range(count + 2):
        top = jnp.maximum(top, jnp.abs(source[first - 1 + i, EDGE : end + EDGE]))
    unit = power_of_two(jnp.maximum(jnp.max(top, axis=0, keepdims=True), 2.0**-60))
    to_whole = jnp.broadcast_to(128.0 / unit, (clat, snaps)).T

    whole = jnp.zeros((snaps, snaps), jnp.int32)
    first_second = jnp.zeros((snaps, snaps), jnp.float32)
    second_any = jnp.zeros((snaps, 2 * snaps), jnp.float32)
    third_any = jnp.zeros((snaps, 2 * snaps), jnp.float32)
    parts = []
    for i in range(count):
        here = first + i
        quarter = tables.quarter[here, EDGE : EDGE + clat]
        along_lon = (quarter * sign) * (source[here + 1, begin:end] - source[here - 1, begin:end])
        along_lat = (quarter * 2.0) * (
            source[here, begin + 1 : end + 1] - source[here, begin - 1 : end - 1]
        )
        for which, value in enumerate((source[here, begin:end], along_lon, along_lat)):
            value = value.T
            planes[which * count + i] = value
            parts.append([piece.astype(jnp.bfloat16) for piece in slices_of(value * to_whole)])
            if len(parts) < DEPTH and not (i == count - 1 and which == 2):
                continue
            a, b, c = [jnp.concatenate(same, axis=1) for same in zip(*parts)]
            parts = []
            from_first = dot_nt(a, jnp.concatenate([a, b], axis=0))
            whole = whole + from_first[:, :snaps].astype(jnp.int32)
            first_second = first_second + from_first[:, snaps:]
            second_any = second_any + dot_nt(b, jnp.concatenate([b, c], axis=0))
            third_any = third_any + dot_nt(c, jnp.concatenate([a, c], axis=0))
    fine = (
        first_second
        + (second_any[:, :snaps] * 0.5 + second_any[:, snaps:])
        + (third_any[:, :snaps] + third_any[:, snaps:] * 0.5)
    )
    head = whole.astype(jnp.float32)
    tail = (whole - head.astype(jnp.int32)).astype(jnp.float32) + (fine + fine.T)
    total = head + tail
    tail = tail - (total - head)
    unit = jnp.broadcast_to(unit * (1.0 / 128.0), (snaps, snaps))
    scale = unit * unit.T
    return total * scale, tail * scale


def add_pairs(left, right):
    total = left[0] + right[0]
    moved = total - left[0]
    lost = (left[0] - (total - moved)) + (right[0] - moved)
    return total, lost + (left[1] + right[1])


def put_gram(gram_ref, head, tail):
    half = head.shape[0] // 2
    for core in range(2):
        gram_ref[core, 0] = head[core * half : (core + 1) * half]
        gram_ref[core, 1] = tail[core * half : (core + 1) * half]


def near_kernel(
    turned_ref, mask_ref, left_ref, right_ref, near_ref, near_left_ref, near_right_ref,
    x_ref, rim_ref, gram_ref,
    field_a, field_b, swept, masks, keep_lon, keep_lat, quarter, *, clon, clat, snaps,
):
    tall = clat + 2 * EDGE
    lower, upper = EDGE, EDGE + tall
    tables = Tables(masks, keep_lon, keep_lat, quarter)
    wide = clon + HALO
    backwards, _, has_left, has_right = place()
    for i in range(HALO):
        ends = ends_of(near_left_ref, near_right_ref, i, has_left, has_right)
        tables.put_masks(HALO - 1 - i, near_ref[HALO * clat + i : HALO * clat + i + 1], *ends[2:])
    for row in range(clon):
        ends = ends_of(left_ref, right_ref, row, has_left, has_right)
        tables.put_masks(HALO + row, mask_ref[row : row + 1], *ends[2:])
    for row in range(wide, masks.shape[1]):
        zero = jnp.zeros((1, clat), jnp.float32)
        tables.put_masks(row, zero, zero, zero)
    tables.fill(range(wide), clat)
    clear_ends(swept, range(wide), tall, snaps)
    for i in range(HALO):
        ends = ends_of(near_left_ref, near_right_ref, i, has_left, has_right)
        start_row(tables, field_a, HALO - 1 - i, ends, near_ref[i * clat : (i + 1) * clat])

    def own_row(row, carry):
        ends = ends_of(left_ref, right_ref, row, has_left, has_right)
        start_row(tables, field_a, row + HALO, ends, turned_ref[row])
        return carry

    lax.fori_loop(0, clon, own_row, 0)
    source, target = field_a, field_b
    for step in range(PASSES + 1):
        rim_ref[step] = source[wide - 2 - step : wide - step, lower:upper]
        if step < PASSES:
            sweep(tables, source, target, swept, step + 1, wide - 1 - step, tall)
            source, target = target, source
    rows = range(clon - HALO)
    put_gram(gram_ref, *fields_and_gram(backwards, tables, source, x_ref, rows, HALO, clat, snaps))


def far_kernel(
    mask_ref, left_ref, right_ref, far_ref, far_left_ref, far_right_ref, rim_ref, gram_in_ref,
    x_ref, gram_ref,
    field_a, field_b, swept, masks, keep_lon, keep_lat, quarter, *, clon, clat, snaps,
):
    tall = clat + 2 * EDGE
    lower, upper = EDGE, EDGE + tall
    tables = Tables(masks, keep_lon, keep_lat, quarter)
    backwards, _, has_left, has_right = place()
    skip = clon - HALO - 1
    wide = 2 * HALO + 1
    for row in range(skip, clon):
        ends = ends_of(left_ref, right_ref, row, has_left, has_right)
        tables.put_masks(row - skip, mask_ref[row : row + 1], *ends[2:])
    for i in range(HALO):
        ends = ends_of(far_left_ref, far_right_ref, i, has_left, has_right)
        tables.put_masks(HALO + 1 + i, far_ref[HALO * clat + i : HALO * clat + i + 1], *ends[2:])
    for row in range(wide, masks.shape[1]):
        zero = jnp.zeros((1, clat), jnp.float32)
        tables.put_masks(row, zero, zero, zero)
    tables.fill(range(1, wide), clat)
    clear_ends(swept, range(1, wide - 1), tall, snaps)
    for i in range(HALO):
        ends = ends_of(far_left_ref, far_right_ref, i, has_left, has_right)
        start_row(tables, field_a, HALO + 1 + i, ends, far_ref[i * clat : (i + 1) * clat])
    source, target = field_a, field_b
    for step in range(PASSES + 1):
        source[HALO - 1 - step : HALO + 1 - step, lower:upper] = rim_ref[step]
        if step < PASSES:
            sweep(tables, source, target, swept, HALO - step, 2 * HALO - step, tall)
            source, target = target, source
    rows = range(clon - HALO, clon)
    gram = fields_and_gram(backwards, tables, source, x_ref, rows, -skip, clat, snaps)
    before = [jnp.concatenate([gram_in_ref[0, part], gram_in_ref[1, part]], axis=0) for part in range(2)]
    put_gram(gram_ref, *add_pairs(before, gram))


def filter_scratch(wide, clat, snaps):
    tall = clat + 2 * EDGE
    field = pltpu.VMEM((wide, tall + 2 * EDGE, snaps), jnp.float32)
    table = pltpu.VMEM((wide, tall, snaps), jnp.float32)
    masks = pltpu.VMEM((3, -(-wide // 8) * 8, clat), jnp.float32)
    return [field, field, field, masks, table, table, table]


def near_part(turned, mask, *halos):
    clon, clat, snaps = turned.shape
    return pl.pallas_call(
        functools.partial(near_kernel, clon=clon, clat=clat, snaps=snaps),
        out_shape=[
            f32(3 * (clon - HALO), snaps, clat),
            f32(PASSES + 1, 2, clat + 2 * EDGE, snaps),
            f32(2, 2, snaps // 2, snaps),
        ],
        in_specs=[VMEM] * 7,
        out_specs=[VMEM, VMEM, VMEM],
        scratch_shapes=filter_scratch(clon + HALO, clat, snaps),
        compiler_params=PARAMS,
        cost_estimate=pl.CostEstimate(flops=4_000_000_000, bytes_accessed=8_000_000, transcendentals=0),
        name="near_part",
    )(turned, mask, *halos)


def far_part(mask, halos, rim, gram, clon, clat, snaps):
    return pl.pallas_call(
        functools.partial(far_kernel, clon=clon, clat=clat, snaps=snaps),
        out_shape=[f32(3 * HALO, snaps, clat), f32(2, 2, snaps // 2, snaps)],
        in_specs=[VMEM] * 8,
        out_specs=[VMEM, VMEM],
        scratch_shapes=filter_scratch(2 * HALO + 1, clat, snaps),
        compiler_params=PARAMS,
        name="far_part",
    )(mask, *halos, rim, gram)


def spread(row, lane):
    return jnp.broadcast_to(row[:, lane : lane + 1], row.shape)


def eliminate(matrix):
    size = matrix.shape[0]
    count = size // 8
    tiles = [matrix[8 * i : 8 * i + 8, :] for i in range(count)]
    lane = lax.broadcasted_iota(jnp.int32, (8, size), 1)
    sub = lax.broadcasted_iota(jnp.int32, (8, size), 0)
    uppers, inverses = [], []

    def every(value, r):
        return jnp.broadcast_to(value[r : r + 1, :], (8, size))

    columns = [spread(tiles[0], c) for c in range(8)]
    for block in range(count):
        base = 8 * block
        panel = tiles[block]
        inside = (lane >= base) & (lane < base + 8)
        rows = [every(panel, r) for r in range(8)]
        entry = {(r, c): every(columns[c], r) for r in range(8) for c in range(r + 1)}
        if block + 1 < count:
            columns = [spread(tiles[block + 1], base + 8 + c) for c in range(8)]
        units = [jnp.where(lane == base + r, 1.0, 0.0) for r in range(8)]
        factor = {}
        pivots = []
        for k in range(8):
            pivots.append(1.0 / entry[k, k])
            for r in range(k + 1, 8):
                factor[r, k] = entry[r, k] * pivots[k]
            for r in range(k + 1, 8):
                for c in range(k + 1, r + 1):
                    entry[r, c] = entry[r, c] - factor[r, k] * entry[c, k]
        for k in range(8):
            for r in range(k + 1, 8):
                rows[r] = rows[r] - factor[r, k] * rows[k]
                units[r] = units[r] - factor[r, k] * units[k]
        joined = [jnp.where(inside, units[r], rows[r]) for r in range(8)]
        for i in range(block + 1, count):
            raw = [spread(tiles[i], base + k) for k in range(8)]
            tile = jnp.where(inside, 0.0, tiles[i])
            for k in range(8):
                scaled = raw[k] * pivots[k]
                for q in range(k + 1, 8):
                    raw[q] = raw[q] - scaled * entry[q, k]
                tile = tile - scaled * joined[k]
                if i == block + 1:
                    columns = [columns[c] - scaled * every(raw[k], c) for c in range(8)]
            tiles[i] = tile
        upper = jnp.zeros((8, size), jnp.float32)
        inverse = jnp.zeros((8, size), jnp.float32)
        for r in range(8):
            scale = lax.rsqrt(entry[r, r])
            upper = jnp.where(sub == r, rows[r] * scale, upper)
            inverse = jnp.where(sub == r, joined[r] * scale, inverse)
        uppers.append(jnp.where(lane >= base + sub, upper, 0.0))
        inverses.append(jnp.where(lane <= base + sub, inverse, 0.0))
    return jnp.concatenate(uppers, axis=0), jnp.concatenate(inverses, axis=0)


def thirds(value):
    first = value.astype(jnp.bfloat16)
    rest = value - first.astype(jnp.float32)
    second = rest.astype(jnp.bfloat16)
    third = (rest - second.astype(jnp.float32)).astype(jnp.bfloat16)
    return first, second, third


def split_kernel(near_ref, far_ref, first_ref, second_ref, third_ref, *, near_rows, far_rows):
    rows = near_rows + far_rows
    for which in range(3):
        for q in range(rows):
            if q < near_rows:
                plane = near_ref[which * near_rows + q]
            else:
                plane = far_ref[which * far_rows + q - near_rows]
            for ref, part in zip((first_ref, second_ref, third_ref), thirds(plane)):
                ref[which * rows + q] = part


def split(x_near, x_far):
    count = x_near.shape[0] + x_far.shape[0]
    part = jax.ShapeDtypeStruct((count, *x_near.shape[1:]), jnp.bfloat16)
    body = functools.partial(split_kernel, near_rows=x_near.shape[0] // 3, far_rows=x_far.shape[0] // 3)
    return pl.pallas_call(
        body,
        out_shape=[part] * 3,
        in_specs=[VMEM] * 2,
        compiler_params=SMALL,
        cost_estimate=pl.CostEstimate(flops=10_000_000, bytes_accessed=2_000_000, transcendentals=0),
        name="split",
    )(x_near, x_far)


def halves(value):
    first = value.astype(jnp.bfloat16)
    return first, (value - first.astype(jnp.float32)).astype(jnp.bfloat16)


def dot_nn_close(left, right):
    (a, b), (c, d) = halves(left), halves(right)
    return dot_nn(jnp.concatenate([a, b], axis=1), jnp.concatenate([c, c], axis=0)) + dot_nn(a, d)


def dot_nt_close(left, right):
    (a, b), (c, d) = halves(left), halves(right)
    return dot_nt(jnp.concatenate([a, b], axis=1), jnp.concatenate([c, c], axis=1)) + dot_nt(a, d)


def modes_kernel(
    gram_ref, first_ref, second_ref, third_ref, modes_ref, factor_ref, out_vmem, upper_vmem, combined_vmem, out_sems, *, clon, clat, snaps, total_rows
):
    head, tail = [jnp.concatenate([gram_ref[0, part], gram_ref[1, part]], axis=0) for part in range(2)]
    row = lax.broadcasted_iota(jnp.int32, (snaps, snaps), 0)
    col = lax.broadcasted_iota(jnp.int32, (snaps, snaps), 1)
    diagonal = jnp.where(row == col, head, 0.0)
    grow = power_of_two(jnp.sqrt(jnp.sum(diagonal, axis=1, keepdims=True)))
    shrink_rows = jnp.broadcast_to(1.0 / grow, (snaps, snaps))
    shrink_cols = shrink_rows.T
    head = head * shrink_rows * shrink_cols
    tail = tail * shrink_rows * shrink_cols

    upper_one, inverse_one = eliminate(head)

    first, second, third = slices_of(upper_one.T * 128.0)
    a = first.astype(jnp.bfloat16)
    b = second.astype(jnp.bfloat16)
    c = third.astype(jnp.bfloat16)
    exact = dot_nt(a, a)
    mixed = dot_nt(a, b)
    mixed_small = dot_nt(a, c) + dot_nt(b, b) * 0.5 + dot_nt(b, c) + dot_nt(c, c) * 0.5
    mixed = mixed + mixed.T
    mixed_small = mixed_small + mixed_small.T
    missing = (head - exact * 2.0**-14) - mixed * 2.0**-14
    missing = missing - mixed_small * 2.0**-14 + tail
    lower_one = (first + second + c.astype(jnp.float32)) * (1.0 / 128.0)

    one = jnp.where(row == col, 1.0, 0.0)
    off = dot_nn(inverse_one, lower_one, HIGHEST) - one
    left_over = dot_nt_close(dot_nn_close(inverse_one, missing), inverse_one)
    difference = (off + off.T) + (dot_nt_close(off, off) + left_over)

    def lower_half(matrix):
        return jnp.where(row > col, matrix, jnp.where(row == col, 0.5 * matrix, 0.0))

    small = jnp.sum(difference * difference) < NEAR_ONE**2

    @pl.when(small)
    def _():
        k = lower_half(difference)
        for _ in range(2):
            rough = k.astype(jnp.bfloat16)
            k = lower_half(difference - dot_nt(rough, rough))
        rough = k.astype(jnp.bfloat16)
        square = dot_nn(rough, rough)
        change = k - dot_nn(rough, (k - square).astype(jnp.bfloat16))
        upper_vmem[...] = k.T + one
        combined_vmem[...] = inverse_one - dot_nn_close(change, inverse_one)

    @pl.when(jnp.logical_not(small))
    def _():
        upper, inverse = eliminate(0.5 * (difference + difference.T) + one)
        upper_vmem[...] = upper
        combined_vmem[...] = dot_nn(inverse, inverse_one, HIGHEST)

    scale = float(total_rows) ** 0.5
    combined = combined_vmem[...] * shrink_cols * scale
    first, second, third = thirds(combined)
    first_second = jnp.concatenate([first, second], axis=1)
    first_third = jnp.concatenate([first, third], axis=1)
    backwards, _, _, _ = place()

    def pair(ref, plane):
        return jnp.concatenate([ref[plane], ref[plane + 1]], axis=1)

    copies = []
    for which in range(3):
        for part in range(clon // 8):
            spot = which * (clon // 8) + part
            flat = out_vmem.at[spot].reshape(snaps * 8, clat)
            for lon in range(0, 8, 2):
                plane = which * clon + part * 8 + lon
                x_one, x_two, x_three = [pair(ref, plane) for ref in (first_ref, second_ref, third_ref)]
                value = (
                    dot_nn(first_third, jnp.concatenate([x_three, x_one], axis=0))
                    + dot_nn(first_second, jnp.concatenate([x_two, x_two], axis=0))
                ) + dot_nn(first_second, jnp.concatenate([x_one, x_one], axis=0))
                for side in range(2):
                    to = longitude(backwards, lon + side, 8)
                    flat[pl.ds(to, snaps, stride=8), :] = value[:, side * clat : (side + 1) * clat]
            to = pl.multiple_of(8 * longitude(backwards, part, clon // 8), 8)
            copy = pltpu.make_async_copy(
                out_vmem.at[spot], modes_ref.at[:, which, pl.ds(to, 8), :], out_sems.at[spot]
            )
            copy.start()
            copies.append(copy)
    lower_two = upper_vmem[...].T
    step = dot_nn_close(off, lower_two)
    lower_two = lower_two - (step - dot_nn_close(off, step))
    factor = dot_nn(lower_two.T, lower_one.T, HIGHEST) * jnp.broadcast_to(grow, (snaps, snaps)).T
    factor_ref[...] = jnp.where(col >= row, factor * (1.0 / scale), 0.0)
    for copy in copies:
        copy.wait()


def orthonormal(gram, x_parts, clon, clat, total_rows):
    snaps = gram.shape[3]
    parts = 3 * clon // 8
    return pl.pallas_call(
        functools.partial(modes_kernel, clon=clon, clat=clat, snaps=snaps, total_rows=total_rows),
        out_shape=[f32(snaps, 3, clon, clat), f32(snaps, snaps)],
        in_specs=[VMEM] * 4,
        out_specs=[ANYWHERE, VMEM],
        scratch_shapes=[
            pltpu.VMEM((parts, snaps, 8, clat), jnp.float32),
            pltpu.VMEM((snaps, snaps), jnp.float32),
            pltpu.VMEM((snaps, snaps), jnp.float32),
            pltpu.SemaphoreType.DMA((parts,)),
        ],
        compiler_params=PARAMS,
        name="orthonormal",
    )(gram, *x_parts)


def summed(halves, nlon, nlat):
    count = nlon * nlat
    core = lax.axis_index("lon") % 2

    def partner(value, step):
        return lax.ppermute(value, BOTH, [(i, i ^ step) for i in range(count)])

    def add(left, right):
        return jnp.stack(add_pairs(left, right))

    mine = add(
        jnp.where(core == 0, halves[0], halves[1]),
        partner(jnp.where(core == 0, halves[1], halves[0]), nlat),
    )
    steps = [1 << bit for bit in range(count.bit_length() - 1) if 1 << bit != nlat]
    while steps:
        if len(steps) >= 2:
            low, high = steps[0], steps[1]
            others = [partner(mine, step) for step in (low, high, low ^ high)]
            mine = add(add(mine, others[0]), add(others[1], others[2]))
            steps = steps[2:]
        else:
            mine = add(mine, partner(mine, steps[0]))
            steps = steps[1:]
    other = partner(mine, nlat)
    return jnp.where(core == 0, jnp.stack([mine, other]), jnp.stack([other, mine]))


def on_device(pressure, ocean_mask):
    snaps, clon, clat = pressure.shape
    nlon, nlat = lax.axis_size("lon"), lax.axis_size("lat")
    merged = nlat == 2
    turned, mask, near, far, ends = prepare(pressure, ocean_mask.astype(jnp.float32), 1 if merged else 2)

    def partner(i, side):
        return [i, i ^ 1, (i + 1 if i % 2 else i - 1) % nlon][side]

    def move(block, side, shift):
        pairs = []
        for i in range(nlon):
            for j in range(nlat):
                to = 1 - j if shift == 0 else j + shift
                if 0 <= to < nlat:
                    pairs.append((i * nlat + j, partner(i, side) * nlat + to))
        return lax.ppermute(block, BOTH, pairs)

    if merged:
        both = [move(ends[side], side, 0) for side in range(3)]
        both = [(block, block) for block in both]
    else:
        both = [(move(ends[3 + side], side, 1), move(ends[side], side, -1)) for side in range(3)]
    far = lax.ppermute(far, "lon", [(i, partner(i, 2)) for i in range(nlon)])
    near = lax.ppermute(near, "lon", [(i, partner(i, 1)) for i in range(nlon)])
    x_near, rim, gram = near_part(turned, mask, *both[0], near, *both[1])
    x_far, gram = far_part(mask, (*both[0], far, *both[2]), rim, gram, clon, clat, snaps)
    x_parts = split(x_near, x_far)
    gram = summed(gram, nlon, nlat)
    return tuple(orthonormal(gram, x_parts, clon, clat, 3 * clon * clat * nlon * nlat))


def solution(mesh):
    return jax.shard_map(
        on_device,
        mesh=mesh,
        in_specs=(P(None, "lon", "lat"), P("lon", "lat")),
        out_specs=(P(None, None, "lon", "lat"), P()),
        check_vma=False,
    )
```
